32 devices in a mesh: parts: 2 (over y), pts: 16 (over z, x, core).
Axes of the slice: x: 2, y: 2, z: 4, core: 2. Of those that a mesh axis runs over, the one named last changes fastest.
Arguments:
- rhs: bfloat16 [32768, 1024], P(('parts', 'pts')), parts along dimension 0, may hold values from -6 to 6
- near_blocks: bfloat16 [128, 12, 256, 256], P(('parts', 'pts')), parts along dimension 0, may hold values from -0.109375 to 0.109375
- near_ids: int32 [128, 12], P(('parts', 'pts')), parts along dimension 0, may hold values from 0 to 63, as said below
- near_count: int32 [128], P(('parts', 'pts')), parts along dimension 0, may hold values from 5 to 12, as said below
- source_basis: bfloat16 [128, 64, 256], P(('parts', 'pts')), parts along dimension 0, may hold values from -0.375 to 0.375
- target_basis: bfloat16 [128, 64, 256], P(('parts', 'pts')), parts along dimension 0, may hold values from -1.5 to 1.5
- leaf_transfer: bfloat16 [128, 64, 64], P(('parts', 'pts')), parts along dimension 0, may hold values from -0.5 to 0.5
- mid_transfer: bfloat16 [64, 64, 64], P(('parts', 'pts')), parts along dimension 0, may hold values from -0.5 to 0.5
- far_coupling: bfloat16 [32, 6, 64, 64], P(('parts', 'pts')), parts along dimension 0, may hold values from -0.3125 to 0.3125
- far_ids: int32 [32, 6], P(('parts', 'pts')), parts along dimension 0, may hold values from 0 to 15, as said below
Outputs:
- product: bfloat16 [32768, 1024], P(('parts', 'pts')), parts along dimension 0
The draws below stay inside these ranges and needn't reach their ends.
There are 2 independent parts, one for each index of `parts`. The reference program is written for one: setup_inputs(seed, part) draws one part's arguments, and reference() takes and returns one part's arrays. A program takes and returns all parts, laid end to end along the dimension named above; each array names one. Nothing has to cross between parts.
Inputs may be any that keep to these rules, and one draw needn't show every extreme that they name: `near_ids`: entry 0 of box b's list is b, entries 0 to 3 are the boxes of b's own group, and the other entries are boxes of the groups at distance 1 to 2 around the loop of 16 groups, distinct within a list. The live entries of the boxes of one group name at most 2 distinct boxes of any other group, and exactly 2 for some pairs of groups. Entries at or after near_count are padding. `near_count`: box b with b % 4 == 0 has all 12 entries live. `far_ids`: each list names distinct groups at distance 3 to 7 around the loop of groups.
All inputs are finite; a program needn't handle non-finite values.
Results may differ from the reference program's by a relative error of at most 0.0041.
Values may be sent and summed in bfloat16 or wider, within the bound.
No kernel may reach another device: no remote copies, remote signals or barrier semaphores. Data moves between devices by JAX's collectives and lax.ppermute only.
A program may use at most 128 MiB of HBM per device.

```python
import jax
import jax.numpy as jnp
from jax import lax

LEAF = 256
RANK = 64
RHS = 1024
B_DEV = 4
REACH = 2
SLOT = 2
NEAR = 12
FARW = 5
FAR = 6
BOXES = 64
POINTS = 16384


def draw_near_ids(key, part):
    key = jax.random.fold_in(key, 11)
    first_key, second_key, third_key = jax.random.split(key, 3)
    groups = BOXES // B_DEV
    box_index = jnp.arange(BOXES, dtype=jnp.int32)
    own_scores = jax.random.randint(first_key, (BOXES, B_DEV), 0, 1024) * B_DEV + jnp.arange(B_DEV, dtype=jnp.int32)[None, :]
    own_scores = jnp.where(jnp.arange(B_DEV, dtype=jnp.int32)[None, :] == (box_index % B_DEV)[:, None], -1, own_scores)
    own_order = jnp.argsort(own_scores, axis=1, stable=True).astype(jnp.int32)
    own_ids = (box_index // B_DEV)[:, None] * B_DEV + own_order
    offsets = jnp.array([radius * sign for radius in range(1, REACH + 1) for sign in (1, -1)], dtype=jnp.int32)
    pick_scores = jax.random.randint(second_key, (groups, 2 * REACH, B_DEV), 0, 1024) * B_DEV + jnp.arange(B_DEV, dtype=jnp.int32)
    picked = jnp.argsort(pick_scores, axis=-1, stable=True)[..., :SLOT].astype(jnp.int32)
    source_group = jnp.mod(jnp.arange(groups, dtype=jnp.int32)[:, None] + offsets[None, :], groups)
    chosen = source_group[:, :, None] * B_DEV + picked
    per_box = chosen[box_index // B_DEV]
    order_scores = jax.random.randint(third_key, (BOXES, 2 * REACH, SLOT), 0, 1024) * SLOT + jnp.arange(SLOT, dtype=jnp.int32)
    order = jnp.argsort(order_scores, axis=-1, stable=True).astype(jnp.int32)
    per_box = jnp.take_along_axis(per_box, order, axis=-1).reshape(BOXES, 2 * REACH * SLOT)
    return jnp.concatenate([own_ids, per_box], axis=1).astype(jnp.int32)


def draw_near_count(key, part):
    key = jax.random.fold_in(key, 12)
    counts = jax.random.randint(key, (BOXES,), B_DEV + 1, NEAR + 1)
    box_index = jnp.arange(BOXES, dtype=jnp.int32)
    return jnp.where(box_index % B_DEV == 0, NEAR, counts).astype(jnp.int32)


def draw_far_ids(key, part):
    key = jax.random.fold_in(key, 13)
    groups = BOXES // B_DEV
    distances = jnp.array([radius * sign for radius in range(REACH + 1, REACH + FARW + 1) for sign in (1, -1)], dtype=jnp.int32)
    scores = jax.random.randint(key, (groups, 2 * FARW), 0, 1024) * (2 * FARW) + jnp.arange(2 * FARW, dtype=jnp.int32)[None, :]
    picked = jnp.argsort(scores, axis=1, stable=True)[:, :FAR].astype(jnp.int32)
    return jnp.mod(jnp.arange(groups, dtype=jnp.int32)[:, None] + distances[picked], groups).astype(jnp.int32)


def levels(rng, extent, cuts, least, largest):
    factor_of, own = 1.0, jax.random.fold_in(rng, 6)
    for dim, shards_of in cuts:
        draws = jnp.exp(jax.random.uniform(jax.random.fold_in(own, dim), (shards_of,), jnp.float32, least / len(cuts), largest / len(cuts)))
        factor_of = factor_of * jnp.repeat(draws, extent[dim] // shards_of).reshape([-1 if axis == dim else 1 for axis in range(len(extent))])
    return factor_of


def noise(own_key, shape, width, most, cuts=(), kind=jnp.bfloat16):
    drawn = jax.random.normal(own_key, shape, jnp.float32) * width
    if len(cuts) > 0:
        drawn = levels(own_key, shape, cuts, -0.22, 0.18) * drawn
    return jnp.clip(drawn, min=-most, max=most).astype(kind)


def setup_inputs(seed: int = 0, part: int = 0) -> dict:
    key_of = jax.random.split(jax.random.key(seed), 11)
    own_keys = jax.random.split(jax.random.fold_in(key_of[10], part), 11)
    rhs = noise(own_keys[0], (POINTS, RHS), 1.0, 6.0, ((0, 16),))
    near_blocks = noise(own_keys[1], (BOXES, NEAR, LEAF, LEAF), (LEAF * NEAR) ** -0.5, 0.109375, ((0, 16),))
    near_ids = draw_near_ids(jax.random.fold_in(jax.random.fold_in(key_of[10], part), 71), part)
    near_count = draw_near_count(jax.random.fold_in(jax.random.fold_in(key_of[10], part), 71), part)
    source_basis = noise(own_keys[4], (BOXES, RANK, LEAF), LEAF ** -0.5, 0.375, ((0, 16),))
    target_basis = noise(own_keys[5], (BOXES, RANK, LEAF), (RANK // 4) ** -0.5, 1.5, ((0, 16),))
    leaf_transfer = noise(own_keys[6], (BOXES, RANK, RANK), (2 * RANK) ** -0.5, 0.5, ((0, 16),))
    mid_transfer = noise(own_keys[7], (BOXES // 2, RANK, RANK), (2 * RANK) ** -0.5, 0.5, ((0, 16),))
    far_coupling = noise(own_keys[8], (BOXES // B_DEV, FAR, RANK, RANK), (RANK * FAR) ** -0.5, 0.3125, ((0, 16),))
    far_ids = draw_far_ids(jax.random.fold_in(jax.random.fold_in(key_of[10], part), 71), part)
    return dict(rhs=rhs, near_blocks=near_blocks, near_ids=near_ids, near_count=near_count, source_basis=source_basis, target_basis=target_basis, leaf_transfer=leaf_transfer, mid_transfer=mid_transfer, far_coupling=far_coupling, far_ids=far_ids)


def reference(rhs, near_blocks, near_ids, near_count, source_basis, target_basis, leaf_transfer, mid_transfer, far_coupling, far_ids):
    highest = lax.Precision.HIGHEST
    leaf_rows = rhs.reshape(BOXES, LEAF, RHS)
    slot_index = jnp.arange(NEAR, dtype=jnp.int32)

    def near_group(group):
        start = (group * B_DEV).astype(jnp.int32)
        list_ids = lax.dynamic_slice_in_dim(near_ids, start, B_DEV, 0)
        counts = lax.dynamic_slice_in_dim(near_count, start, B_DEV, 0)
        blocks = lax.dynamic_slice_in_dim(near_blocks, start, B_DEV, 0)
        live = slot_index[None, :] < counts[:, None]
        gathered = jnp.where(live[:, :, None, None], leaf_rows[list_ids], jnp.zeros((), leaf_rows.dtype))
        return jnp.einsum("bnij,bnjr->bir", blocks.astype(jnp.float32), gathered.astype(jnp.float32))

    groups = jnp.arange(BOXES // B_DEV, dtype=jnp.int32)
    near_part = lax.map(near_group, groups).reshape(BOXES, LEAF, RHS)
    leaf_coef = jnp.einsum("bkl,blr->bkr", source_basis.astype(jnp.float32), leaf_rows.astype(jnp.float32))
    mid_coef = jnp.einsum("bpk,bkr->bpr", leaf_transfer.astype(jnp.float32), leaf_coef, precision=highest)
    mid_coef = mid_coef.reshape(BOXES // 2, 2, RANK, RHS).sum(axis=1)
    top_coef = jnp.einsum("bpk,bkr->bpr", mid_transfer.astype(jnp.float32), mid_coef, precision=highest)
    panel = top_coef.reshape(BOXES // B_DEV, 2, RANK, RHS).sum(axis=1).astype(jnp.bfloat16)
    chosen = panel[far_ids]
    coupled = jnp.einsum("gfpq,gfqr->gpr", far_coupling.astype(jnp.float32), chosen.astype(jnp.float32))
    mid_down = jnp.einsum("kab,kar->kbr", mid_transfer.astype(jnp.float32), jnp.repeat(coupled, 2, axis=0), precision=highest)
    leaf_down = jnp.einsum("jab,jar->jbr", leaf_transfer.astype(jnp.float32), jnp.repeat(mid_down, 2, axis=0), precision=highest)
    far_part = jnp.einsum("jkl,jkr->jlr", target_basis.astype(jnp.float32), leaf_down, precision=highest)
    return (near_part + far_part).reshape(BOXES * LEAF, RHS).astype(jnp.bfloat16)
```

```python
import functools

import jax
import jax.numpy as jnp
from jax import lax
from jax.experimental import pallas as pl
from jax.experimental.pallas import tpu as pltpu
from jax.sharding import PartitionSpec as P

LEAF = 256
RANK = 64
B_DEV = 4
NEAR = 12
ROWS = B_DEV * LEAF
PIECES = 5
SLABS = ((0, 256), (256, 256), (512, 256), (768, 128), (896, 128))
SLOTS = ((3, 4, 0, 1, 2), (3, 1, 0, 4, 2), (2, 4, 0, 1, 3), (2, 1, 0, 4, 3))
MIB = 1024 * 1024


def split(value):
    high = value.astype(jnp.bfloat16)
    low = (value - high.astype(jnp.float32)).astype(jnp.bfloat16)
    return high, low


def dot(a, b):
    return jnp.dot(a, b, preferred_element_type=jnp.float32)


def dot32(a, b):
    return jnp.dot(
        a.astype(jnp.float32),
        b.astype(jnp.float32),
        precision=lax.Precision.HIGHEST,
        preferred_element_type=jnp.float32,
    )


def up_kernel(rhs_ref, source_ref, target_ref, leaf_ref, mid_ref, panel_ref, down_ref):
    ups = []
    for box in range(B_DEV):
        chain = dot32(mid_ref[box // 2], leaf_ref[box])
        ups.append(dot32(chain, source_ref[box]))
        high, low = split(dot32(chain, target_ref[box]).T)
        down_ref[box] = jnp.concatenate([high, low, high], axis=1)
    high, low = split(jnp.concatenate(ups, axis=1))
    both = dot(jnp.concatenate([high, low], axis=0), rhs_ref[...])
    panel_ref[...] = (both[:RANK] + both[RANK:]).astype(jnp.bfloat16)


def up(rhs, source_basis, target_basis, leaf_transfer, mid_transfer):
    columns = rhs.shape[1]
    return pl.pallas_call(
        up_kernel,
        out_shape=(
            jax.ShapeDtypeStruct((RANK, columns), jnp.bfloat16),
            jax.ShapeDtypeStruct((B_DEV, LEAF, 3 * RANK), jnp.bfloat16),
        ),
        compiler_params=pltpu.CompilerParams(vmem_limit_bytes=24 * MIB),
        cost_estimate=pl.CostEstimate(
            flops=2 * 2 * RANK * ROWS * columns, bytes_accessed=4 * MIB, transcendentals=0
        ),
    )(rhs, source_basis, target_basis, leaf_transfer, mid_transfer)


def slab_kernel(
    start,
    width,
    entry_ref,
    far_ref,
    near_ref,
    own_ref,
    core_ref,
    across_ref,
    along_ref,
    other_ref,
    panels_ref,
    coupling_ref,
    down_ref,
    *rest,
):
    out_ref, held, chosen, coupled, sems = rest[-5:]
    far = far_ref.shape[0]
    box = pl.program_id(0)

    @pl.when(box == 0)
    def _():
        columns = pl.ds(start, width)
        copies = [
            pltpu.make_async_copy(
                panels_ref.at[far_ref[f], :, columns], chosen.at[pl.ds(f * RANK, RANK)], sems.at[PIECES + f]
            )
            for f in range(far)
        ]
        for piece, ref in enumerate((own_ref, core_ref, across_ref, along_ref, other_ref)):
            source = ref.at[:, columns] if piece < 2 else ref
            copies.append(
                pltpu.make_async_copy(source, held.at[pl.ds(piece * ROWS, ROWS)], sems.at[piece])
            )
        for copy in copies:
            copy.start()
        held[pl.ds(PIECES * ROWS, LEAF)] = jnp.zeros((LEAF, width), jnp.bfloat16)
        for copy in copies:
            copy.wait()
        high, low = split(
            dot(jnp.concatenate([coupling_ref[f] for f in range(far)], axis=1), chosen[...])
        )
        coupled[...] = jnp.concatenate([high, high, low], axis=0)

    total = dot(down_ref[0], coupled[...])
    left = jnp.concatenate([near_ref[0, n] for n in range(NEAR)], axis=1)
    right = jnp.concatenate(
        [held[pl.ds(pl.multiple_of(entry_ref[box, n] * LEAF, LEAF), LEAF)] for n in range(NEAR)], axis=0
    )
    out_ref[...] = (total + dot(left, right)).astype(jnp.bfloat16)


def slab(start, width, entry, far_list, near_blocks, pieces, panels, coupling, down, product):
    rows, columns = pieces[0].shape
    far = far_list.shape[0]
    anywhere = pl.BlockSpec(memory_space=pl.ANY)
    in_specs = [
        pl.BlockSpec((1, NEAR, LEAF, LEAF), lambda b, *_: (b, 0, 0, 0)),
        *[anywhere] * (PIECES + 1),
        pl.BlockSpec((far, RANK, RANK), lambda b, *_: (0, 0, 0)),
        pl.BlockSpec((1, LEAF, 3 * RANK), lambda b, *_: (b, 0, 0)),
    ]
    operands = [near_blocks, *pieces, panels, coupling, down]
    aliases = {}
    if product is not None:
        aliases = {2 + len(operands): 0}
        in_specs.append(anywhere)
        operands.append(product)
    return pl.pallas_call(
        functools.partial(slab_kernel, start, width),
        grid_spec=pltpu.PrefetchScalarGridSpec(
            num_scalar_prefetch=2,
            grid=(B_DEV,),
            in_specs=in_specs,
            out_specs=pl.BlockSpec((LEAF, width), lambda b, *_: (b, start // width)),
            scratch_shapes=[
                pltpu.VMEM((PIECES * ROWS + LEAF, width), jnp.bfloat16),
                pltpu.VMEM((far * RANK, width), jnp.bfloat16),
                pltpu.VMEM((3 * RANK, width), jnp.bfloat16),
                pltpu.SemaphoreType.DMA((PIECES + far,)),
            ],
        ),
        out_shape=jax.ShapeDtypeStruct((rows, columns), jnp.bfloat16),
        input_output_aliases=aliases,
        compiler_params=pltpu.CompilerParams(vmem_limit_bytes=24 * MIB),
        cost_estimate=pl.CostEstimate(
            flops=2 * B_DEV * NEAR * LEAF * LEAF * width, bytes_accessed=10 * MIB, transcendentals=0
        ),
    )(entry, far_list, *operands)


def on_device(
    rhs,
    near_blocks,
    near_ids,
    near_count,
    source_basis,
    target_basis,
    leaf_transfer,
    mid_transfer,
    far_coupling,
    far_ids,
):
    members = lax.axis_size("pts")
    position = lax.axis_index("pts")
    across_pairs = [(i, i ^ 2) for i in range(members)]
    core_pairs = [(i, i ^ 1) for i in range(members)]
    along_pairs = [(i, (i + (-4 if i & 2 else 4)) % members) for i in range(members)]

    across = [lax.ppermute(rhs[:, start : start + width], "pts", across_pairs) for start, width in SLABS]
    core = lax.ppermute(rhs, "pts", core_pairs)
    panel, down = up(rhs, source_basis, target_basis, leaf_transfer, mid_transfer)
    panels = lax.all_gather(panel, "pts")

    distance = jnp.mod(near_ids // B_DEV - position + 2, members)
    slots = jnp.asarray(SLOTS, jnp.int32)[position % 4]
    held_in = sum(jnp.where(distance == d, slots[d], 0) for d in range(5))
    live = jnp.arange(NEAR, dtype=jnp.int32)[None, :] < near_count[:, None]
    entry = jnp.where(live, held_in * B_DEV + near_ids % B_DEV, PIECES * B_DEV)

    sends_across = (position % 4 == 0) | (position % 4 == 3)
    product = None
    for (start, width), arrived in zip(SLABS, across):
        along = lax.ppermute(arrived, "pts", along_pairs)
        other = lax.ppermute(jnp.where(sends_across, arrived, along), "pts", core_pairs)
        product = slab(
            start,
            width,
            entry,
            far_ids[0],
            near_blocks,
            (rhs, core, arrived, along, other),
            panels,
            far_coupling[0],
            down,
            product,
        )
    return product


def solution(mesh):
    return jax.shard_map(
        on_device,
        mesh=mesh,
        in_specs=(
            P(("parts", "pts"), None),
            P(("parts", "pts"), None, None, None),
            P(("parts", "pts"), None),
            P(("parts", "pts")),
            P(("parts", "pts"), None, None),
            P(("parts", "pts"), None, None),
            P(("parts", "pts"), None, None),
            P(("parts", "pts"), None, None),
            P(("parts", "pts"), None, None, None),
            P(("parts", "pts"), None),
        ),
        out_specs=P(("parts", "pts"), None),
        check_vma=False,
    )
```

```python
import functools

import jax
import jax.numpy as jnp
from jax import lax
from jax.experimental import pallas as pl
from jax.experimental.pallas import tpu as pltpu
from jax.sharding import PartitionSpec as P

LEAF = 256
RANK = 64
B_DEV = 4
NEAR = 12
ROWS = B_DEV * LEAF
SLABS = ((0, 256), (256, 256), (512, 256), (768, 128), (896, 128))
OWN, CORE, ACROSS, ACROSS_CORE, ALONG, ALONG_CORE, ZERO = 0, 4, 8, 12, 16, 18, 20
HELD = 21
HELD_AT = (
    (ALONG, ALONG_CORE, OWN, CORE, ACROSS),
    (ALONG, CORE, OWN, ACROSS_CORE, ACROSS),
    (ACROSS, ACROSS_CORE, OWN, CORE, ALONG),
    (ACROSS, CORE, OWN, ALONG_CORE, ALONG),
)
MIB = 1024 * 1024
ANYWHERE = pl.BlockSpec(memory_space=pl.ANY)
VECTOR = pl.BlockSpec(memory_space=pltpu.VMEM)
SCALAR = pl.BlockSpec(memory_space=pltpu.SMEM)


def cost(mib):
    return pl.CostEstimate(flops=1024, bytes_accessed=mib * MIB, transcendentals=0)


def split(value):
    high = value.astype(jnp.bfloat16)
    low = (value - high.astype(jnp.float32)).astype(jnp.bfloat16)
    return high, low


def dot(a, b):
    return jnp.dot(a, b, preferred_element_type=jnp.float32)


def dot32(a, b):
    return jnp.dot(
        a.astype(jnp.float32),
        b.astype(jnp.float32),
        precision=lax.Precision.HIGHEST,
        preferred_element_type=jnp.float32,
    )


def cut_kernel(rhs_any, *rest):
    parts, sems = rest[:-1], rest[-1]
    copies = [
        pltpu.make_async_copy(rhs_any.at[:, pl.ds(start, width)], part, sems.at[k])
        for k, ((start, width), part) in enumerate(zip(SLABS, parts))
    ]
    for copy in copies:
        copy.start()
    for copy in copies:
        copy.wait()


def cut(rhs):
    return pl.pallas_call(
        cut_kernel,
        in_specs=[ANYWHERE],
        out_shape=tuple(jax.ShapeDtypeStruct((ROWS, width), rhs.dtype) for _, width in SLABS),
        scratch_shapes=[pltpu.SemaphoreType.DMA((len(SLABS),))],
        compiler_params=pltpu.CompilerParams(vmem_limit_bytes=16 * MIB),
        cost_estimate=cost(4),
    )(rhs)


def first_two(mask):
    first = jnp.where(mask & 1 != 0, 0, jnp.where(mask & 2 != 0, 1, jnp.where(mask & 4 != 0, 2, 3)))
    mask = mask & (mask - 1)
    second = jnp.where(mask & 2 != 0, 1, jnp.where(mask & 4 != 0, 2, 3))
    return first, second


def plan(members, ids_ref, count_ref, entry_ref, wish_refs):
    position = lax.axis_index("pts")
    kind = position & 3
    held_at = []
    for d in range(5):
        at = jnp.int32(HELD_AT[0][d])
        for other in range(1, 4):
            at = jnp.where(kind == other, HELD_AT[other][d], at)
        held_at.append(at)
    masks = [jnp.int32(0), jnp.int32(0)]
    bases = {}
    for box in range(B_DEV):
        live = count_ref[box]
        for n in range(NEAR):
            number = ids_ref[box, n]
            distance = (number >> 2) - position + 2
            distance = jnp.where(distance < 0, distance + members, distance)
            distance = jnp.where(distance >= members, distance - members, distance)
            base = held_at[0]
            for d in range(1, 5):
                base = jnp.where(distance == d, held_at[d], base)
            base = jnp.where(n < live, base, ZERO)
            bit = jnp.int32(1) << (number & 3)
            masks[0] = masks[0] | jnp.where(base == ALONG, bit, 0)
            masks[1] = masks[1] | jnp.where(base == ALONG_CORE, bit, 0)
            bases[box, n] = (base, number & 3)
    picks = [first_two(mask) for mask in masks]
    for (box, n), (base, inner) in bases.items():
        first = jnp.where(base == ALONG, picks[0][0], picks[1][0])
        inner = jnp.where(base == ZERO, 0, jnp.where(base >= ALONG, jnp.where(inner == first, 0, 1), inner))
        entry_ref[box, n] = base + inner
    for (first, second), wish_ref in zip(picks, wish_refs):
        lane = lax.broadcasted_iota(jnp.int32, wish_ref.shape, 1)
        wish_ref[...] = jnp.where(lane == 0, first, second)


def up_kernel(
    reach,
    members,
    source_any,
    target_any,
    leaf_any,
    mid_any,
    coupling_any,
    far_any,
    count_any,
    ids_any,
    *rest,
):
    parts = rest[: len(SLABS)]
    panel_ref, down_ref, placed_ref, partner_placed_ref, entry_ref, wish_ref, core_wish_ref = rest[len(SLABS) : -9]
    source_ref, target_ref, leaf_ref, mid_ref, coupling_ref, far_ref, count_ref, ids_ref, sems = rest[-9:]
    pairs = (
        (leaf_any, leaf_ref),
        (mid_any, mid_ref),
        (source_any, source_ref),
        (far_any, far_ref),
        (count_any, count_ref),
        (ids_any, ids_ref),
        (target_any, target_ref),
        (coupling_any, coupling_ref),
    )
    copies = [pltpu.make_async_copy(a, b, sems.at[i]) for i, (a, b) in enumerate(pairs)]
    for copy in copies:
        copy.start()
    for copy in copies:
        copy.wait()
    chains = [dot32(mid_ref[box // 2], leaf_ref[box]) for box in range(B_DEV)]
    ups = [dot32(chains[box], source_ref[box]) for box in range(B_DEV)]
    high, low = split(jnp.concatenate(ups, axis=1))
    both = jnp.concatenate([high, low], axis=0)
    for (start, width), part in zip(SLABS, parts):
        sums = dot(both, part[...])
        panel_ref[:, pl.ds(start, width)] = (sums[:RANK] + sums[RANK:]).astype(jnp.bfloat16)
    for box in range(B_DEV):
        high, low = split(dot32(chains[box], target_ref[box]).T)
        down_ref[box] = jnp.concatenate([high, low, high], axis=1)
    plan(members, ids_ref, count_ref, entry_ref, (wish_ref, core_wish_ref))
    position = lax.axis_index("pts")
    quad, side, core = position >> 2, (position >> 1) & 1, position & 1
    for half, ref in enumerate((placed_ref, partner_placed_ref)):
        blocks = []
        for other in range(2):
            for step in reach:
                held_quad = quad + step
                held_quad = jnp.where(held_quad >= members // 4, held_quad - members // 4, held_quad)
                group = held_quad * 4 + 2 * (side ^ half) + (core ^ other)
                block = jnp.zeros((RANK, RANK), jnp.float32)
                for f in range(coupling_ref.shape[0]):
                    block = jnp.where(far_ref[0, f] == group, coupling_ref[f].astype(jnp.float32), block)
                blocks.append(block)
        ref[...] = jnp.concatenate(blocks, axis=1).astype(jnp.bfloat16)


def up(reach, members, parts, arrays, far_ids, near_count, near_ids):
    columns = sum(width for _, width in SLABS)
    placed = jax.ShapeDtypeStruct((RANK, 2 * len(reach) * RANK), jnp.bfloat16)
    wish = jax.ShapeDtypeStruct((1, 128), jnp.int32)
    return pl.pallas_call(
        functools.partial(up_kernel, reach, members),
        in_specs=[ANYWHERE] * 8 + [VECTOR] * len(parts),
        out_specs=(VECTOR,) * 4 + (SCALAR,) + (VECTOR,) * 2,
        out_shape=(
            jax.ShapeDtypeStruct((RANK, columns), jnp.bfloat16),
            jax.ShapeDtypeStruct((B_DEV, LEAF, 3 * RANK), jnp.bfloat16),
            placed,
            placed,
            jax.ShapeDtypeStruct(near_ids.shape, jnp.int32),
            wish,
            wish,
        ),
        scratch_shapes=[pltpu.VMEM(a.shape, a.dtype) for a in arrays]
        + [pltpu.SMEM(a.shape, jnp.int32) for a in (far_ids, near_count, near_ids)]
        + [pltpu.SemaphoreType.DMA((8,))],
        compiler_params=pltpu.CompilerParams(vmem_limit_bytes=32 * MIB),
        cost_estimate=cost(512),
    )(*arrays, far_ids, near_count, near_ids, *parts)


def couple_kernel(mine_ref, core_ref, own_ref, partner_ref, own_sum_ref, partner_sum_ref):
    table = jnp.concatenate([mine_ref[...], core_ref[...]], axis=0)
    partner_sum_ref[...] = dot(partner_ref[...], table)
    own_sum_ref[...] = dot(own_ref[...], table)


def couple(mine, core, own, partner):
    shape = jax.ShapeDtypeStruct((RANK, mine.shape[1]), jnp.float32)
    return pl.pallas_call(
        couple_kernel,
        out_shape=(shape, shape),
        compiler_params=pltpu.CompilerParams(vmem_limit_bytes=16 * MIB),
        cost_estimate=cost(1),
    )(mine, core, own, partner)


def pack_kernel(wish_ref, core_wish_ref, arrived_ref, along_ref, along_core_ref):
    for wishes, picked_ref in ((wish_ref, along_ref), (core_wish_ref, along_core_ref)):
        for k in range(2):
            rows = pl.ds(pl.multiple_of(wishes[0, k] * LEAF, LEAF), LEAF)
            picked_ref[pl.ds(k * LEAF, LEAF)] = arrived_ref[rows]


def pack(wish, core_wish, arrived):
    shape = jax.ShapeDtypeStruct((2 * LEAF, arrived.shape[1]), arrived.dtype)
    return pl.pallas_call(
        pack_kernel,
        in_specs=[SCALAR, SCALAR, VECTOR],
        out_shape=(shape, shape),
        compiler_params=pltpu.CompilerParams(vmem_limit_bytes=8 * MIB),
        cost_estimate=cost(1),
    )(wish, core_wish, arrived)


def near_kernel(start, entry_ref, near_ref, own_ref, core_ref, across_ref, across_core_ref, along_ref, along_core_ref, sum_ref, held):
    width = sum_ref.shape[1]
    pieces = (
        (OWN, own_ref),
        (CORE, core_ref.at[:, pl.ds(start, width)]),
        (ACROSS, across_ref),
        (ACROSS_CORE, across_core_ref),
        (ALONG, along_ref),
        (ALONG_CORE, along_core_ref),
    )
    for at, ref in pieces:
        held[pl.ds(at * LEAF, ref.shape[0])] = ref[...]
    held[pl.ds(ZERO * LEAF, LEAF)] = jnp.zeros((LEAF, width), jnp.bfloat16)
    for box in range(B_DEV):
        left = [near_ref[box, n] for n in range(NEAR)]
        right = [held[pl.ds(pl.multiple_of(entry_ref[box, n] * LEAF, LEAF), LEAF)] for n in range(NEAR)]
        sum_ref[pl.ds(box * LEAF, LEAF)] = dot(
            jnp.concatenate(left, axis=1), jnp.concatenate(right, axis=0)
        )


def near(start, width, entry, near_blocks, pieces):
    return pl.pallas_call(
        functools.partial(near_kernel, start),
        in_specs=[SCALAR] + [VECTOR] * (1 + len(pieces)),
        out_specs=VECTOR,
        scratch_shapes=[pltpu.VMEM((HELD * LEAF, width), jnp.bfloat16)],
        out_shape=jax.ShapeDtypeStruct((ROWS, width), jnp.float32),
        compiler_params=pltpu.CompilerParams(vmem_limit_bytes=24 * MIB),
        cost_estimate=cost(8),
    )(entry, near_blocks, *pieces)


def finish_kernel(slabs, own_sum_ref, partner_sum_ref, down_ref, *rest):
    sum_refs = rest[: len(slabs)]
    out_ref, made, sems = rest[-3:]
    start, stop = slabs[0][0], slabs[-1][0] + slabs[-1][1]
    taken = pl.ds(start, stop - start)
    high, low = split(own_sum_ref[:, taken] + partner_sum_ref[:, taken])
    coupled = jnp.concatenate([high, high, low], axis=0)
    copies = []
    for box in range(B_DEV):
        rows = pl.ds(box * LEAF, LEAF)
        far = dot(down_ref[box], coupled)
        for (at, width), sum_ref in zip(slabs, sum_refs):
            columns = slice(at - start, at - start + width)
            made[rows, columns] = (far[:, columns] + sum_ref[rows]).astype(jnp.bfloat16)
        copy = pltpu.make_async_copy(made.at[rows], out_ref.at[rows, taken], sems.at[box])
        copy.start()
        copies.append(copy)
    for copy in copies:
        copy.wait()


def finish(slabs, sums, down, nears, product):
    columns = sums[0].shape[1]
    operands = [*sums, down, *nears]
    in_specs = [VECTOR] * len(operands)
    aliases = {}
    if product is not None:
        aliases = {len(operands): 0}
        in_specs.append(ANYWHERE)
        operands.append(product)
    return pl.pallas_call(
        functools.partial(finish_kernel, slabs),
        in_specs=in_specs,
        out_specs=ANYWHERE,
        scratch_shapes=[
            pltpu.VMEM((ROWS, sum(width for _, width in slabs)), jnp.bfloat16),
            pltpu.SemaphoreType.DMA((B_DEV,)),
        ],
        out_shape=jax.ShapeDtypeStruct((ROWS, columns), jnp.bfloat16),
        input_output_aliases=aliases,
        compiler_params=pltpu.CompilerParams(vmem_limit_bytes=24 * MIB),
        cost_estimate=cost(4),
    )(*operands)


def on_device(
    rhs,
    near_blocks,
    near_ids,
    near_count,
    source_basis,
    target_basis,
    leaf_transfer,
    mid_transfer,
    far_coupling,
    far_ids,
):
    members = lax.axis_size("pts")
    every = range(members)
    across_pairs = [(i, i ^ 2) for i in every]
    core_pairs = [(i, i ^ 1) for i in every]
    along_pairs = [(i, (i + (-4 if i & 2 else 4)) % members) for i in every]
    along_core_pairs = [(i, (i + (-3 if i & 2 else 3)) % members) for i in every if i % 4 in (1, 2)]
    back = lambda pairs: [(b, a) for a, b in pairs]
    permute = lambda value, pairs: lax.ppermute(value, "pts", pairs)
    meet = lambda *values: lax.optimization_barrier(values)
    reach = sorted({step % (members // 4) for step in range(-2, 3)})
    count = len(SLABS)

    parts = list(cut(rhs))
    across = [permute(part, across_pairs) for part in parts[:2]]
    panel, down, placed, partner_placed, entry, wish, core_wish = up(
        reach,
        members,
        parts,
        (source_basis, target_basis, leaf_transfer, mid_transfer, far_coupling[0]),
        far_ids,
        near_count,
        near_ids,
    )
    wish = permute(wish, back(along_pairs))
    core_wish = permute(core_wish, back(along_core_pairs))
    others = [permute(panel, [(i, (i - 4 * step) % members) for i in every]) for step in reach[1:]]
    rhs_core = permute(rhs, core_pairs)
    partner_placed = permute(partner_placed, across_pairs)

    across_core, along, nears = [], [], []

    def relay(k):
        picked, core_picked = pack(wish, core_wish, across[k])
        along.append((permute(picked, along_pairs), permute(core_picked, along_core_pairs)))
        across_core.append(permute(across[k], core_pairs))

    def multiply(k):
        pieces = (parts[k], rhs_core, across[k], across_core[k], *along[k])
        nears.append(near(*SLABS[k], entry, near_blocks, pieces))

    across[0], panel, parts[2], wish, core_wish, *others = meet(
        across[0], panel, parts[2], wish, core_wish, *others
    )
    across.append(permute(parts[2], across_pairs))
    relay(0)
    mine = jnp.concatenate([panel, *others], axis=0)
    mine_core = permute(mine, core_pairs)

    along[0] = list(along[0])
    across[1], parts[3], along[0][0], along[0][1], mine_core, partner_placed = meet(
        across[1], parts[3], *along[0], mine_core, partner_placed
    )
    across.append(permute(parts[3], across_pairs))
    relay(1)
    own_sum, partner_sum = couple(mine, mine_core, placed, partner_placed)

    across[2], parts[4], across_core[0], partner_sum, *along[1] = meet(
        across[2], parts[4], across_core[0], partner_sum, *along[1]
    )
    across.append(permute(parts[4], across_pairs))
    relay(2)
    multiply(0)

    across[3], across_core[1], partner_sum, nears[0] = meet(across[3], across_core[1], partner_sum, nears[0])
    relay(3)
    partner_sum = permute(partner_sum, across_pairs)
    multiply(1)

    across[4], across_core[2], nears[1], *along[2] = meet(across[4], across_core[2], nears[1], *along[2])
    relay(4)
    multiply(2)
    multiply(3)
    sums = (own_sum, partner_sum)
    product = finish(SLABS[:-1], sums, down, nears, None)
    multiply(4)
    return finish(SLABS[-1:], sums, down, nears[-1:], product)


def solution(mesh):
    return jax.shard_map(
        on_device,
        mesh=mesh,
        in_specs=(
            P(("parts", "pts"), None),
            P(("parts", "pts"), None, None, None),
            P(("parts", "pts"), None),
            P(("parts", "pts")),
            P(("parts", "pts"), None, None),
            P(("parts", "pts"), None, None),
            P(("parts", "pts"), None, None),
            P(("parts", "pts"), None, None),
            P(("parts", "pts"), None, None, None),
            P(("parts", "pts"), None),
        ),
        out_specs=P(("parts", "pts"), None),
        check_vma=False,
    )
```

```python
import functools

import jax
import jax.numpy as jnp
from jax import lax
from jax.experimental import pallas as pl
from jax.experimental.pallas import tpu as pltpu
from jax.sharding import PartitionSpec as P

LEAF = 256
RANK = 64
B_DEV = 4
NEAR = 12
ROWS = B_DEV * LEAF
SLABS = ((0, 256), (256, 256), (512, 256), (768, 256))
CARRIER = 2
WISH = 16
OWN, CORE, ACROSS, ACROSS_CORE, ALONG, ALONG_CORE, ZERO = 0, 4, 8, 12, 16, 18, 20
HELD = 21
HELD_AT = (
    (ALONG, ALONG_CORE, OWN, CORE, ACROSS),
    (ALONG, CORE, OWN, ACROSS_CORE, ACROSS),
    (ACROSS, ACROSS_CORE, OWN, CORE, ALONG),
    (ACROSS, CORE, OWN, ALONG_CORE, ALONG),
)
MIB = 1024 * 1024
ANYWHERE = pl.BlockSpec(memory_space=pl.ANY)
VECTOR = pl.BlockSpec(memory_space=pltpu.VMEM)
SCALAR = pl.BlockSpec(memory_space=pltpu.SMEM)


def cost(mib):
    return pl.CostEstimate(flops=1024, bytes_accessed=mib * MIB, transcendentals=0)


def split(value):
    high = value.astype(jnp.bfloat16)
    low = (value - high.astype(jnp.float32)).astype(jnp.bfloat16)
    return high, low


def dot(a, b):
    return jnp.dot(a, b, preferred_element_type=jnp.float32)


def dot32(a, b):
    return jnp.dot(
        a.astype(jnp.float32),
        b.astype(jnp.float32),
        precision=lax.Precision.HIGHEST,
        preferred_element_type=jnp.float32,
    )


def cut_kernel(rhs_any, *rest):
    parts, sems = rest[:-1], rest[-1]
    copies = [
        pltpu.make_async_copy(rhs_any.at[:, pl.ds(start, width)], part.at[pl.ds(0, ROWS)], sems.at[k])
        for k, ((start, width), part) in enumerate(zip(SLABS, parts))
    ]
    for copy in copies:
        copy.start()
    for copy in copies:
        copy.wait()


def cut(rhs, carried):
    shapes = [(ROWS, width) for _, width in SLABS]
    shapes[CARRIER] = (ROWS + RANK * -(-carried // SLABS[CARRIER][1]), SLABS[CARRIER][1])
    return pl.pallas_call(
        cut_kernel,
        in_specs=[ANYWHERE],
        out_shape=tuple(jax.ShapeDtypeStruct(shape, rhs.dtype) for shape in shapes),
        scratch_shapes=[pltpu.SemaphoreType.DMA((len(SLABS),))],
        compiler_params=pltpu.CompilerParams(vmem_limit_bytes=16 * MIB),
        cost_estimate=cost(4),
    )(rhs)


def first_two(named):
    first = jnp.where(named[0], 0, jnp.where(named[1], 1, jnp.where(named[2], 2, 3)))
    second = jnp.where(named[1] & (first < 1), 1, jnp.where(named[2] & (first < 2), 2, 3))
    return first, second


def places(members, position, lists):
    numbers = lists[:, :NEAR]
    distance = (numbers >> 2) - position + 2
    distance = jnp.where(distance < 0, distance + members, distance)
    distance = jnp.where(distance >= members, distance - members, distance)
    base = jnp.full(numbers.shape, ZERO, jnp.int32)
    for d in range(5):
        at = jnp.int32(HELD_AT[0][d])
        for kind in range(1, 4):
            at = jnp.where(position & 3 == kind, HELD_AT[kind][d], at)
        base = jnp.where(distance == d, at, base)
    live = lax.broadcasted_iota(jnp.int32, numbers.shape, 1) < lists[:, NEAR:]
    base = jnp.where(live, base, ZERO)
    inner = numbers & 3
    picks = []
    for group in (ALONG, ALONG_CORE):
        named = []
        for box in range(B_DEV):
            here = jnp.where((base == group) & (inner == box), 1, 0)
            named.append(jnp.max(jnp.max(here, axis=1, keepdims=True), axis=0, keepdims=True) > 0)
        picks.append(first_two(named))
    return base, inner, picks


def up_kernel(members, source_any, leaf_any, mid_any, lists_ref, core_lists_ref, *rest):
    parts = rest[: len(SLABS)]
    panel_ref, entry_ref, source_ref, leaf_ref, mid_ref, sems = rest[len(SLABS) :]
    pairs = ((leaf_any, leaf_ref), (mid_any, mid_ref), (source_any, source_ref))
    copies = [pltpu.make_async_copy(a, b, sems.at[i]) for i, (a, b) in enumerate(pairs)]
    for copy in copies:
        copy.start()
    position = lax.axis_index("pts")
    base, inner, (picks, core_side_picks) = places(members, position, lists_ref[...])
    first = jnp.where(base == ALONG, picks[0], core_side_picks[0])
    picked = jnp.where(inner == first, 0, 1)
    entry_ref[...] = base + jnp.where(base == ZERO, 0, jnp.where(base >= ALONG, picked, inner))
    _, _, (_, partner_picks) = places(members, position ^ 1, core_lists_ref[...])
    quarter = panel_ref.shape[1] // 4
    for k, name in enumerate((*picks, *partner_picks)):
        panel_ref[pl.ds(RANK, WISH), pl.ds(k * quarter, quarter)] = jnp.broadcast_to(
            name.astype(jnp.float32), (WISH, quarter)
        ).astype(jnp.bfloat16)
    for copy in copies:
        copy.wait()
    ups = [dot32(dot32(mid_ref[box // 2], leaf_ref[box]), source_ref[box]) for box in range(B_DEV)]
    high, low = split(jnp.concatenate(ups, axis=1))
    both = jnp.concatenate([high, low], axis=0)
    for (start, width), part in zip(SLABS, parts):
        sums = dot(both, part[pl.ds(0, ROWS)])
        panel_ref[pl.ds(0, RANK), pl.ds(start, width)] = (sums[:RANK] + sums[RANK:]).astype(jnp.bfloat16)


def up(members, parts, source_basis, leaf_transfer, mid_transfer, lists, core_lists):
    columns = sum(width for _, width in SLABS)
    arrays = (source_basis, leaf_transfer, mid_transfer)
    return pl.pallas_call(
        functools.partial(up_kernel, members),
        in_specs=[ANYWHERE] * 3 + [VECTOR] * (2 + len(parts)),
        out_shape=(
            jax.ShapeDtypeStruct((RANK + WISH, columns), jnp.bfloat16),
            jax.ShapeDtypeStruct((B_DEV, NEAR), jnp.int32),
        ),
        scratch_shapes=[pltpu.VMEM(a.shape, a.dtype) for a in arrays] + [pltpu.SemaphoreType.DMA((3,))],
        compiler_params=pltpu.CompilerParams(vmem_limit_bytes=16 * MIB),
        cost_estimate=cost(512),
    )(*arrays, lists, core_lists, *parts)


def down_kernel(reach, members, far_ref, target_ref, leaf_ref, mid_ref, coupling_ref, part_in, part_ref, down_ref, placed_ref):
    for box in range(B_DEV):
        chain = dot32(mid_ref[box // 2], leaf_ref[box])
        high, low = split(dot32(chain, target_ref[box]).T)
        down_ref[box] = jnp.concatenate([high, low, high], axis=1)
    position = lax.axis_index("pts")
    quad, side, core = position >> 2, (position >> 1) & 1, position & 1
    for half in range(2):
        blocks = []
        for other in range(2):
            for step in reach:
                held_quad = quad + step
                held_quad = jnp.where(held_quad >= members // 4, held_quad - members // 4, held_quad)
                group = held_quad * 4 + 2 * (side ^ half) + (core ^ other)
                block = jnp.zeros((RANK, RANK), jnp.float32)
                for f in range(coupling_ref.shape[0]):
                    block = jnp.where(far_ref[0, f] == group, coupling_ref[f].astype(jnp.float32), block)
                blocks.append(block)
        placed = jnp.concatenate(blocks, axis=1).astype(jnp.bfloat16)
        if half == 0:
            placed_ref[...] = placed
            continue
        width = part_ref.shape[1]
        for line, at in enumerate(range(0, placed.shape[1], width)):
            taken = placed[:, at : at + width]
            part_ref[pl.ds(ROWS + line * RANK, RANK), pl.ds(0, taken.shape[1])] = taken


def down(reach, members, far_ids, target_basis, leaf_transfer, mid_transfer, coupling, part):
    return pl.pallas_call(
        functools.partial(down_kernel, reach, members),
        in_specs=[SCALAR] + [VECTOR] * 5,
        out_specs=(VECTOR,) * 3,
        out_shape=(
            jax.ShapeDtypeStruct(part.shape, part.dtype),
            jax.ShapeDtypeStruct((B_DEV, LEAF, 3 * RANK), jnp.bfloat16),
            jax.ShapeDtypeStruct((RANK, 2 * len(reach) * RANK), jnp.bfloat16),
        ),
        input_output_aliases={5: 0},
        compiler_params=pltpu.CompilerParams(vmem_limit_bytes=16 * MIB),
        cost_estimate=cost(1),
    )(far_ids, target_basis, leaf_transfer, mid_transfer, coupling, part)


def wishes_kernel(behind_ref, ahead_ref, wish_ref):
    forth = (lax.axis_index("pts") & 2) == 0
    quarter = behind_ref.shape[1] // 4
    for k in range(4):
        at = (pl.ds(RANK, WISH), pl.ds(k * quarter, 128))
        value = jnp.where(forth, ahead_ref[at].astype(jnp.float32), behind_ref[at].astype(jnp.float32))
        wish_ref[0, k] = jnp.max(value).astype(jnp.int32)


def wishes(behind, ahead):
    return pl.pallas_call(
        wishes_kernel,
        in_specs=[VECTOR, VECTOR],
        out_specs=SCALAR,
        out_shape=jax.ShapeDtypeStruct((1, 4), jnp.int32),
        compiler_params=pltpu.CompilerParams(vmem_limit_bytes=8 * MIB),
        cost_estimate=cost(1),
    )(behind, ahead)


def couple_kernel(own_ref, carrier_ref, *rest):
    tables, (own_sum_ref, partner_sum_ref) = rest[:-2], rest[-2:]
    depth = own_ref.shape[1]
    table = jnp.concatenate([ref[pl.ds(0, RANK)] for ref in tables], axis=0)
    lines = [carrier_ref[pl.ds(row, RANK)] for row in range(ROWS, carrier_ref.shape[0], RANK)]
    partner_sum_ref[...] = dot(jnp.concatenate(lines, axis=1)[:, :depth], table)
    own_sum_ref[...] = dot(own_ref[...], table)


def couple(own, carrier, tables):
    shape = jax.ShapeDtypeStruct((RANK, tables[0].shape[1]), jnp.float32)
    return pl.pallas_call(
        couple_kernel,
        out_shape=(shape, shape),
        compiler_params=pltpu.CompilerParams(vmem_limit_bytes=16 * MIB),
        cost_estimate=cost(1),
    )(own, carrier, *tables)


def pack_kernel(wish_ref, arrived_ref, along_ref, along_core_ref):
    for side, picked_ref in enumerate((along_ref, along_core_ref)):
        for k in range(2):
            rows = pl.ds(pl.multiple_of(wish_ref[0, 2 * side + k] * LEAF, LEAF), LEAF)
            picked_ref[pl.ds(k * LEAF, LEAF)] = arrived_ref[rows]


def pack(wish, arrived):
    shape = jax.ShapeDtypeStruct((2 * LEAF, arrived.shape[1]), arrived.dtype)
    return pl.pallas_call(
        pack_kernel,
        in_specs=[SCALAR, VECTOR],
        out_shape=(shape, shape),
        compiler_params=pltpu.CompilerParams(vmem_limit_bytes=8 * MIB),
        cost_estimate=cost(1),
    )(wish, arrived)


def gather(start, width, held, pieces):
    own_ref, core_ref, across_ref, across_core_ref, along_ref, along_core_ref = pieces
    for at, ref, boxes in (
        (OWN, own_ref, B_DEV),
        (CORE, core_ref.at[:, pl.ds(start, width)], B_DEV),
        (ACROSS, across_ref, B_DEV),
        (ACROSS_CORE, across_core_ref, B_DEV),
        (ALONG, along_ref, 2),
        (ALONG_CORE, along_core_ref, 2),
    ):
        held[pl.ds(at * LEAF, boxes * LEAF)] = ref[pl.ds(0, boxes * LEAF)]
    held[pl.ds(ZERO * LEAF, LEAF)] = jnp.zeros((LEAF, width), jnp.bfloat16)


def operands(box, entry_ref, near_ref, held):
    left = [near_ref[box, n] for n in range(NEAR)]
    right = [held[pl.ds(pl.multiple_of(entry_ref[box, n] * LEAF, LEAF), LEAF)] for n in range(NEAR)]
    return left, right


def near_kernel(start, entry_ref, near_ref, *rest):
    pieces, (sum_ref, held) = rest[:-2], rest[-2:]
    gather(start, sum_ref.shape[1], held, pieces)
    for box in range(B_DEV):
        left, right = operands(box, entry_ref, near_ref, held)
        sum_ref[pl.ds(box * LEAF, LEAF)] = dot(
            jnp.concatenate(left, axis=1), jnp.concatenate(right, axis=0)
        )


def near(start, width, entry, near_blocks, pieces):
    return pl.pallas_call(
        functools.partial(near_kernel, start),
        in_specs=[SCALAR] + [VECTOR] * (1 + len(pieces)),
        out_specs=VECTOR,
        scratch_shapes=[pltpu.VMEM((HELD * LEAF, width), jnp.bfloat16)],
        out_shape=jax.ShapeDtypeStruct((ROWS, width), jnp.float32),
        compiler_params=pltpu.CompilerParams(vmem_limit_bytes=16 * MIB),
        cost_estimate=cost(8),
    )(entry, near_blocks, *pieces)


def last_kernel(start, width, entry_ref, near_ref, own_sum_ref, partner_sum_ref, down_ref, *rest):
    pieces, (_, out_ref, held, made, sems) = rest[:-5], rest[-5:]
    gather(start, width, held, pieces)
    taken = pl.ds(start, width)
    high, low = split(own_sum_ref[:, taken] + partner_sum_ref[:, taken])
    coupled = jnp.concatenate([high, high, low], axis=0)
    copies = []
    for box in range(B_DEV):
        left, right = operands(box, entry_ref, near_ref, held)
        rows = pl.ds(box * LEAF, LEAF)
        near_sum = dot(jnp.concatenate(left, axis=1), jnp.concatenate(right, axis=0))
        made[rows] = (near_sum + dot(down_ref[box], coupled)).astype(jnp.bfloat16)
        copy = pltpu.make_async_copy(made.at[rows], out_ref.at[rows, taken], sems.at[box])
        copy.start()
        copies.append(copy)
    for copy in copies:
        copy.wait()


def last(start, width, entry, near_blocks, sums, down_basis, pieces, product):
    given = [entry, near_blocks, *sums, down_basis, *pieces, product]
    return pl.pallas_call(
        functools.partial(last_kernel, start, width),
        in_specs=[SCALAR] + [VECTOR] * (len(given) - 2) + [ANYWHERE],
        out_specs=ANYWHERE,
        scratch_shapes=[
            pltpu.VMEM((HELD * LEAF, width), jnp.bfloat16),
            pltpu.VMEM((ROWS, width), jnp.bfloat16),
            pltpu.SemaphoreType.DMA((B_DEV,)),
        ],
        out_shape=jax.ShapeDtypeStruct(product.shape, product.dtype),
        input_output_aliases={len(given) - 1: 0},
        compiler_params=pltpu.CompilerParams(vmem_limit_bytes=16 * MIB),
        cost_estimate=cost(8),
    )(*given)


def finish_kernel(slabs, own_sum_ref, partner_sum_ref, down_ref, *rest):
    sum_refs = rest[: len(slabs)]
    out_ref, made, sems = rest[-3:]
    start, stop = slabs[0][0], slabs[-1][0] + slabs[-1][1]
    taken = pl.ds(start, stop - start)
    high, low = split(own_sum_ref[:, taken] + partner_sum_ref[:, taken])
    coupled = jnp.concatenate([high, high, low], axis=0)
    copies = []
    for box in range(B_DEV):
        rows = pl.ds(box * LEAF, LEAF)
        far = dot(down_ref[box], coupled)
        for (at, width), sum_ref in zip(slabs, sum_refs):
            columns = slice(at - start, at - start + width)
            made[rows, columns] = (far[:, columns] + sum_ref[rows]).astype(jnp.bfloat16)
        copy = pltpu.make_async_copy(made.at[rows], out_ref.at[rows, taken], sems.at[box])
        copy.start()
        copies.append(copy)
    for copy in copies:
        copy.wait()


def finish(slabs, sums, down_basis, nears):
    columns = sums[0].shape[1]
    given = [*sums, down_basis, *nears]
    return pl.pallas_call(
        functools.partial(finish_kernel, slabs),
        in_specs=[VECTOR] * len(given),
        out_specs=ANYWHERE,
        scratch_shapes=[
            pltpu.VMEM((ROWS, sum(width for _, width in slabs)), jnp.bfloat16),
            pltpu.SemaphoreType.DMA((B_DEV,)),
        ],
        out_shape=jax.ShapeDtypeStruct((ROWS, columns), jnp.bfloat16),
        compiler_params=pltpu.CompilerParams(vmem_limit_bytes=16 * MIB),
        cost_estimate=cost(4),
    )(*given)


def on_device(
    rhs,
    near_blocks,
    near_ids,
    near_count,
    source_basis,
    target_basis,
    leaf_transfer,
    mid_transfer,
    far_coupling,
    far_ids,
):
    members = lax.axis_size("pts")
    every = range(members)
    across_pairs = [(i, i ^ 2) for i in every]
    core_pairs = [(i, i ^ 1) for i in every]
    along_pairs = [(i, (i + (-4 if i & 2 else 4)) % members) for i in every]
    along_core_pairs = [(i, (i + (-3 if i & 2 else 3)) % members) for i in every if i % 4 in (1, 2)]
    permute = lambda value, pairs: lax.ppermute(value, "pts", pairs)
    meet = lambda *values: lax.optimization_barrier(values)
    quads = members // 4
    reach = sorted({step % quads for step in range(-2, 3)})

    lists = jnp.concatenate([near_ids, near_count[:, None]], axis=1)
    core_lists = permute(lists, core_pairs)
    rhs_core = permute(rhs, core_pairs)
    parts = list(cut(rhs, 2 * len(reach) * RANK))
    panel, entry = up(members, parts, source_basis, leaf_transfer, mid_transfer, lists, core_lists)
    parts[CARRIER], down_basis, placed = down(
        reach, members, far_ids, target_basis, leaf_transfer, mid_transfer, far_coupling[0], parts[CARRIER]
    )
    across = [permute(part, across_pairs) for part in parts]
    others = [permute(panel, [(i, (i - 4 * step) % members) for i in every]) for step in reach[1:]]

    across_core, along, nears = [], [], []

    def relay(k):
        picked, core_picked = pack(wish, across[k])
        along.append([permute(picked, along_pairs), permute(core_picked, along_core_pairs)])
        across_core.append(permute(across[k], core_pairs))

    def pieces(k):
        return (parts[k], rhs_core, across[k], across_core[k], *along[k])

    def multiply(k):
        nears.append(near(*SLABS[k], entry, near_blocks, pieces(k)))

    behind, ahead = reach.index(quads - 1) - 1, reach.index(1) - 1
    across[0], panel, others[behind], others[ahead] = meet(across[0], panel, others[behind], others[ahead])
    wish = wishes(others[behind], others[ahead])
    relay(0)

    across[1], along[0][0], panel, *others = meet(across[1], along[0][0], panel, *others)
    relay(1)

    across[2], across_core[0], panel, along[0][1], along[1][0] = meet(
        across[2], across_core[0], panel, along[0][1], along[1][0]
    )
    relay(2)
    multiply(0)
    mine = [panel, *others]
    own_sum, partner_sum = couple(placed, across[2], mine + [permute(each, core_pairs) for each in mine])

    across[3], across_core[1], partner_sum, nears[0], along[1][1], along[2][0] = meet(
        across[3], across_core[1], partner_sum, nears[0], along[1][1], along[2][0]
    )
    relay(3)
    partner_sum = permute(partner_sum, across_pairs)
    multiply(1)
    multiply(2)
    sums = (own_sum, partner_sum)
    product = finish(SLABS[:-1], sums, down_basis, nears)
    product, *along[3] = meet(product, *along[3])
    return last(*SLABS[3], entry, near_blocks, sums, down_basis, pieces(3), product)


def solution(mesh):
    return jax.shard_map(
        on_device,
        mesh=mesh,
        in_specs=(
            P(("parts", "pts"), None),
            P(("parts", "pts"), None, None, None),
            P(("parts", "pts"), None),
            P(("parts", "pts")),
            P(("parts", "pts"), None, None),
            P(("parts", "pts"), None, None),
            P(("parts", "pts"), None, None),
            P(("parts", "pts"), None, None),
            P(("parts", "pts"), None, None, None),
            P(("parts", "pts"), None),
        ),
        out_specs=P(("parts", "pts"), None),
        check_vma=False,
    )
```

```python
import functools

import jax
import jax.numpy as jnp
from jax import lax
from jax.experimental import pallas as pl
from jax.experimental.pallas import tpu as pltpu
from jax.sharding import PartitionSpec as P

LEAF = 256
RANK = 64
B_DEV = 4
NEAR = 12
ROWS = B_DEV * LEAF
SLABS = ((0, 256), (256, 256), (512, 256), (768, 256))
CARRIER = 2
WISH = 16
OWN, CORE, ACROSS, ACROSS_CORE, ALONG, ALONG_CORE, ZERO = 0, 4, 8, 12, 14, 16, 18
HELD = 19
HELD_AT = (
    (ALONG, ALONG_CORE, OWN, CORE, ACROSS),
    (ALONG, CORE, OWN, ACROSS_CORE, ACROSS),
    (ACROSS, ACROSS_CORE, OWN, CORE, ALONG),
    (ACROSS, CORE, OWN, ALONG_CORE, ALONG),
)
MIB = 1024 * 1024
STEP = 0.4
UP_LIMIT = 58
BYTES = 1
ANYWHERE = pl.BlockSpec(memory_space=pl.ANY)
VECTOR = pl.BlockSpec(memory_space=pltpu.VMEM)
SCALAR = pl.BlockSpec(memory_space=pltpu.SMEM)


def cost(microseconds):
    return pl.CostEstimate(flops=int(microseconds * 1.15e9), bytes_accessed=BYTES * MIB, transcendentals=0)


def split(value):
    high = value.astype(jnp.bfloat16)
    low = (value - high.astype(jnp.float32)).astype(jnp.bfloat16)
    return high, low


def dot(a, b):
    return jnp.dot(a, b, preferred_element_type=jnp.float32)


def dot_split(a, b):
    high, low = split(a)
    both = dot(jnp.concatenate([high, low], axis=0), b)
    return both[: a.shape[0]] + both[a.shape[0] :]


def first_two(named):
    first = jnp.where(named[0], 0, jnp.where(named[1], 1, jnp.where(named[2], 2, 3)))
    second = jnp.where(named[1] & (first < 1), 1, jnp.where(named[2] & (first < 2), 2, 3))
    return first, second


def places(members, position, numbers, counts):
    distance = (numbers >> 2) - position + 2
    distance = jnp.where(distance < 0, distance + members, distance)
    distance = jnp.where(distance >= members, distance - members, distance)
    base = jnp.full(numbers.shape, ZERO, jnp.int32)
    for d in range(5):
        at = jnp.int32(HELD_AT[0][d])
        for kind in range(1, 4):
            at = jnp.where(position & 3 == kind, HELD_AT[kind][d], at)
        base = jnp.where(distance == d, at, base)
    row = lax.broadcasted_iota(jnp.int32, (B_DEV, B_DEV), 0)
    column = lax.broadcasted_iota(jnp.int32, (B_DEV, B_DEV), 1)
    counts = jnp.max(jnp.where(row == column, counts, 0), axis=1, keepdims=True)
    live = lax.broadcasted_iota(jnp.int32, numbers.shape, 1) < counts
    base = jnp.where(live, base, ZERO)
    inner = numbers & 3
    picks = []
    for group in (ALONG, ALONG_CORE, ACROSS_CORE):
        named = []
        for box in range(B_DEV):
            here = jnp.where((base == group) & (inner == box), 1, 0)
            named.append(jnp.max(jnp.max(here, axis=1, keepdims=True), axis=0, keepdims=True) > 0)
        picks.append(first_two(named))
    return base, inner, picks


def up_kernel(members, *refs):
    given, rest = refs[:6], refs[6:]
    panel_ref, entry_ref, *parts = rest[: 2 + len(SLABS)]
    *kept, sems = rest[2 + len(SLABS) :]
    pairs = list(zip(given[:5], kept))
    pairs += [(given[5].at[:, pl.ds(start, width)], part.at[pl.ds(0, ROWS)]) for (start, width), part in zip(SLABS, parts)]
    copies = [pltpu.make_async_copy(a, b, sems.at[i]) for i, (a, b) in enumerate(pairs)]
    for copy in copies:
        copy.start()
    source_ref, leaf_ref, mid_ref, ids_ref, count_ref = kept
    for copy in copies[:5]:
        copy.wait()
    base, inner, picks = places(members, lax.axis_index("pts"), ids_ref[...], count_ref[...])
    first = jnp.where(base == ALONG, picks[0][0], jnp.where(base == ALONG_CORE, picks[1][0], picks[2][0]))
    picked = jnp.where(inner == first, 0, 1)
    entry_ref[...] = base + jnp.where(base == ZERO, 0, jnp.where(base >= ACROSS_CORE, picked, inner))
    for k, name in enumerate(pick[n] for pick in picks for n in range(2)):
        panel_ref[pl.ds(RANK, WISH), pl.ds(k * 128, 128)] = jnp.broadcast_to(
            name.astype(jnp.float32), (WISH, 128)
        ).astype(jnp.bfloat16)
    panel_ref[pl.ds(RANK, WISH), pl.ds(6 * 128, 2 * 128)] = jnp.zeros((WISH, 2 * 128), jnp.bfloat16)
    ups = [dot_split(dot(mid_ref[box // 2], leaf_ref[box]), source_ref[box]) for box in range(B_DEV)]
    high, low = split(jnp.concatenate(ups, axis=1))
    both = jnp.concatenate([high, low], axis=0)
    for copy, (start, width), part in zip(copies[5:], SLABS, parts):
        copy.wait()
        sums = dot(both, part[pl.ds(0, ROWS)])
        panel_ref[pl.ds(0, RANK), pl.ds(start, width)] = (sums[:RANK] + sums[RANK:]).astype(jnp.bfloat16)


def up(members, carried, *given):
    columns = given[-1].shape[1]
    shapes = [(ROWS, width) for _, width in SLABS]
    shapes[CARRIER] = (ROWS + RANK * -(-carried // shapes[CARRIER][1]), shapes[CARRIER][1])
    return pl.pallas_call(
        functools.partial(up_kernel, members),
        in_specs=[ANYWHERE] * len(given),
        out_shape=(
            jax.ShapeDtypeStruct((RANK + WISH, columns), jnp.bfloat16),
            jax.ShapeDtypeStruct((B_DEV, NEAR), jnp.int32),
            *[jax.ShapeDtypeStruct(shape, jnp.bfloat16) for shape in shapes],
        ),
        scratch_shapes=[pltpu.VMEM(a.shape, a.dtype) for a in given[:5]]
        + [pltpu.SemaphoreType.DMA((5 + len(SLABS),))],
        compiler_params=pltpu.CompilerParams(vmem_limit_bytes=UP_LIMIT * MIB),
        cost_estimate=cost(2),
        name="up",
    )(*given)


def down_kernel(reach, members, far_ref, target_ref, leaf_ref, mid_ref, coupling_ref, *rest):
    part_ref, down_ref, placed_ref, lines_ref, sem = rest[-5:]
    for box in range(B_DEV):
        chain = dot(mid_ref[box // 2], leaf_ref[box])
        high, low = split(dot_split(chain, target_ref[box]).T)
        down_ref[box] = jnp.concatenate([high, low, high], axis=1)
    position = lax.axis_index("pts")
    quad, side, core = position >> 2, (position >> 1) & 1, position & 1
    for half in range(2):
        blocks = []
        for other in range(2):
            for step in reach:
                held_quad = quad + step
                held_quad = jnp.where(held_quad >= members // 4, held_quad - members // 4, held_quad)
                group = held_quad * 4 + 2 * (side ^ half) + (core ^ other)
                block = jnp.zeros((RANK, RANK), jnp.float32)
                for f in range(coupling_ref.shape[0]):
                    block = jnp.where(far_ref[0, f] == group, coupling_ref[f].astype(jnp.float32), block)
                blocks.append(block)
        placed = jnp.concatenate(blocks, axis=1).astype(jnp.bfloat16)
        if half == 0:
            placed_ref[...] = placed
            continue
        width = part_ref.shape[1]
        for line, at in enumerate(range(0, placed.shape[1], width)):
            taken = placed[:, at : at + width]
            lines_ref[pl.ds(line * RANK, RANK), pl.ds(0, taken.shape[1])] = taken
        copy = pltpu.make_async_copy(lines_ref, part_ref.at[pl.ds(ROWS, lines_ref.shape[0])], sem)
        copy.start()
        copy.wait()


def down(reach, members, far_ids, target_basis, leaf_transfer, mid_transfer, coupling, part, *before):
    return pl.pallas_call(
        functools.partial(down_kernel, reach, members),
        in_specs=[SCALAR] + [VECTOR] * 4 + [ANYWHERE] * (1 + len(before)),
        out_specs=(ANYWHERE, VECTOR, VECTOR),
        out_shape=(
            jax.ShapeDtypeStruct(part.shape, part.dtype),
            jax.ShapeDtypeStruct((B_DEV, LEAF, 3 * RANK), jnp.bfloat16),
            jax.ShapeDtypeStruct((RANK, 2 * len(reach) * RANK), jnp.bfloat16),
        ),
        scratch_shapes=[
            pltpu.VMEM((part.shape[0] - ROWS, part.shape[1]), part.dtype),
            pltpu.SemaphoreType.DMA,
        ],
        input_output_aliases={5: 0},
        compiler_params=pltpu.CompilerParams(vmem_limit_bytes=16 * MIB),
        cost_estimate=cost(1),
        name="down",
    )(far_ids, target_basis, leaf_transfer, mid_transfer, coupling, part, *before)


def ask_kernel(panel_ref, ahead_ref, behind_ref, *rest):
    asked_ref = rest[-1]
    forth = (lax.axis_index("pts") & 2) == 0
    wishes = (pl.ds(RANK, WISH), pl.ds(0, 6 * 128))
    ahead, behind = ahead_ref[wishes].astype(jnp.float32), behind_ref[wishes].astype(jnp.float32)
    asked_ref[pl.ds(0, WISH)] = jnp.where(forth, ahead, behind).astype(jnp.bfloat16)
    asked_ref[pl.ds(WISH, WISH)] = panel_ref[wishes]


def ask(panel, ahead, behind, *before):
    return pl.pallas_call(
        ask_kernel,
        in_specs=[VECTOR] * 3 + [ANYWHERE] * len(before),
        out_shape=jax.ShapeDtypeStruct((2 * WISH, 6 * 128), jnp.bfloat16),
        compiler_params=pltpu.CompilerParams(vmem_limit_bytes=8 * MIB),
        cost_estimate=cost(0.1),
        name="ask",
    )(panel, ahead, behind, *before)


def wishes_kernel(asked_ref, core_asked_ref, wish_ref):
    for name in range(6):
        ref = asked_ref if name < 2 else core_asked_ref
        value = ref[pl.ds(0 if name < 4 else WISH, WISH), pl.ds(name * 128, 128)]
        wish_ref[0, name] = jnp.max(value.astype(jnp.float32)).astype(jnp.int32)


def wishes(asked, core_asked):
    return pl.pallas_call(
        wishes_kernel,
        in_specs=[VECTOR] * 2,
        out_specs=SCALAR,
        out_shape=jax.ShapeDtypeStruct((1, 6), jnp.int32),
        compiler_params=pltpu.CompilerParams(vmem_limit_bytes=8 * MIB),
        cost_estimate=cost(0.1),
        name="wishes",
    )(asked, core_asked)


def couple_kernel(own_ref, carrier_ref, *rest):
    tables, (own_sum_ref, partner_sum_ref) = rest[:-2], rest[-2:]
    depth = own_ref.shape[1]
    table = jnp.concatenate([ref[...] for ref in tables], axis=0)
    lines = [carrier_ref[pl.ds(row, RANK)] for row in range(ROWS, carrier_ref.shape[0], RANK)]
    partner_sum_ref[...] = dot(jnp.concatenate(lines, axis=1)[:, :depth], table)
    own_sum_ref[...] = dot(own_ref[...], table)


def couple(own, carrier, *tables):
    shape = jax.ShapeDtypeStruct((RANK, tables[0].shape[1]), jnp.float32)
    return pl.pallas_call(
        couple_kernel,
        out_shape=(shape, shape),
        compiler_params=pltpu.CompilerParams(vmem_limit_bytes=16 * MIB),
        cost_estimate=cost(0.1),
        name="couple",
    )(own, carrier, *tables)


def pick(wish_ref, at, arrived_ref, picked_ref):
    for k in range(2):
        rows = pl.ds(pl.multiple_of(wish_ref[0, at + k] * LEAF, LEAF), LEAF)
        picked_ref[pl.ds(k * LEAF, LEAF)] = arrived_ref[rows]


def pack_kernel(wish_ref, arrived_ref, *rest):
    for at, picked_ref in enumerate(rest[-3:]):
        pick(wish_ref, 2 * at, arrived_ref, picked_ref)


def pack(wish, arrived, before):
    shape = jax.ShapeDtypeStruct((2 * LEAF, arrived.shape[1]), arrived.dtype)
    return pl.pallas_call(
        pack_kernel,
        in_specs=[SCALAR, VECTOR] + [ANYWHERE] * len(before),
        out_shape=(shape,) * 3,
        compiler_params=pltpu.CompilerParams(vmem_limit_bytes=8 * MIB),
        cost_estimate=cost(0.02),
        name="pack",
    )(wish, arrived, *before)


def gather(start, width, held, pieces):
    own_ref, core_ref, across_ref, across_core_ref, along_ref, along_core_ref = pieces
    for at, boxes, taken in (
        (OWN, B_DEV, own_ref[pl.ds(0, ROWS)]),
        (CORE, B_DEV, core_ref[:, pl.ds(start, width)]),
        (ACROSS, B_DEV, across_ref[pl.ds(0, ROWS)]),
        (ACROSS_CORE, 2, across_core_ref[...]),
        (ALONG, 2, along_ref[...]),
        (ALONG_CORE, 2, along_core_ref[...]),
    ):
        held[pl.ds(at * LEAF, boxes * LEAF)] = taken
    held[pl.ds(ZERO * LEAF, LEAF)] = jnp.zeros((LEAF, width), jnp.bfloat16)


def operands(box, entry_ref, near_ref, held):
    left = [near_ref[box, n] for n in range(NEAR)]
    right = [held[pl.ds(pl.multiple_of(entry_ref[box, n] * LEAF, LEAF), LEAF)] for n in range(NEAR)]
    return left, right


def near_kernel(start, entry_ref, near_ref, *rest):
    pieces, (sum_ref, held) = rest[:6], rest[-2:]
    gather(start, sum_ref.shape[1], held, pieces)
    for box in range(B_DEV):
        left, right = operands(box, entry_ref, near_ref, held)
        sum_ref[pl.ds(box * LEAF, LEAF)] = dot(
            jnp.concatenate(left, axis=1), jnp.concatenate(right, axis=0)
        )


def near(start, width, entry, near_blocks, pieces, before):
    return pl.pallas_call(
        functools.partial(near_kernel, start),
        in_specs=[SCALAR] + [VECTOR] * (1 + len(pieces)) + [ANYWHERE] * len(before),
        out_specs=VECTOR,
        scratch_shapes=[pltpu.VMEM((HELD * LEAF, width), jnp.bfloat16)],
        out_shape=jax.ShapeDtypeStruct((ROWS, width), jnp.float32),
        compiler_params=pltpu.CompilerParams(vmem_limit_bytes=16 * MIB),
        cost_estimate=cost(STEP),
        name="near",
    )(entry, near_blocks, *pieces, *before)


def last_kernel(start, width, entry_ref, near_ref, own_sum_ref, partner_sum_ref, down_ref, *rest):
    pieces, (_, out_ref, held, made, sems) = rest[:-5], rest[-5:]
    gather(start, width, held, pieces)
    taken = pl.ds(start, width)
    high, low = split(own_sum_ref[:, taken] + partner_sum_ref[:, taken])
    coupled = jnp.concatenate([high, high, low], axis=0)
    copies = []
    for box in range(B_DEV):
        left, right = operands(box, entry_ref, near_ref, held)
        rows = pl.ds(box * LEAF, LEAF)
        near_sum = dot(jnp.concatenate(left, axis=1), jnp.concatenate(right, axis=0))
        made[rows] = (near_sum + dot(down_ref[box], coupled)).astype(jnp.bfloat16)
        copy = pltpu.make_async_copy(made.at[rows], out_ref.at[rows, taken], sems.at[box])
        copy.start()
        copies.append(copy)
    for copy in copies:
        copy.wait()


def last(start, width, entry, near_blocks, sums, down_basis, pieces, product):
    given = [entry, near_blocks, *sums, down_basis, *pieces, product]
    return pl.pallas_call(
        functools.partial(last_kernel, start, width),
        in_specs=[SCALAR] + [VECTOR] * (len(given) - 2) + [ANYWHERE],
        out_specs=ANYWHERE,
        scratch_shapes=[
            pltpu.VMEM((HELD * LEAF, width), jnp.bfloat16),
            pltpu.VMEM((ROWS, width), jnp.bfloat16),
            pltpu.SemaphoreType.DMA((B_DEV,)),
        ],
        out_shape=jax.ShapeDtypeStruct(product.shape, product.dtype),
        input_output_aliases={len(given) - 1: 0},
        compiler_params=pltpu.CompilerParams(vmem_limit_bytes=16 * MIB),
        cost_estimate=cost(1),
        name="last",
    )(*given)


def finish_kernel(slabs, own_sum_ref, partner_sum_ref, down_ref, *rest):
    sum_refs = rest[: len(slabs)]
    out_ref, made, sems = rest[-3:]
    start, stop = slabs[0][0], slabs[-1][0] + slabs[-1][1]
    taken = pl.ds(start, stop - start)
    high, low = split(own_sum_ref[:, taken] + partner_sum_ref[:, taken])
    coupled = jnp.concatenate([high, high, low], axis=0)
    copies = []
    for box in range(B_DEV):
        rows = pl.ds(box * LEAF, LEAF)
        far = dot(down_ref[box], coupled)
        for (at, width), sum_ref in zip(slabs, sum_refs):
            columns = slice(at - start, at - start + width)
            made[rows, columns] = (far[:, columns] + sum_ref[rows]).astype(jnp.bfloat16)
        copy = pltpu.make_async_copy(made.at[rows], out_ref.at[rows, taken], sems.at[box])
        copy.start()
        copies.append(copy)
    for copy in copies:
        copy.wait()


def finish(slabs, sums, down_basis, nears):
    columns = sums[0].shape[1]
    given = [*sums, down_basis, *nears]
    return pl.pallas_call(
        functools.partial(finish_kernel, slabs),
        in_specs=[VECTOR] * len(given),
        out_specs=ANYWHERE,
        scratch_shapes=[
            pltpu.VMEM((ROWS, sum(width for _, width in slabs)), jnp.bfloat16),
            pltpu.SemaphoreType.DMA((B_DEV,)),
        ],
        out_shape=jax.ShapeDtypeStruct((ROWS, columns), jnp.bfloat16),
        compiler_params=pltpu.CompilerParams(vmem_limit_bytes=16 * MIB),
        cost_estimate=cost(STEP),
        name="finish",
    )(*given)


def on_device(
    rhs,
    near_blocks,
    near_ids,
    near_count,
    source_basis,
    target_basis,
    leaf_transfer,
    mid_transfer,
    far_coupling,
    far_ids,
):
    members = lax.axis_size("pts")
    every = range(members)
    across_pairs = [(i, i ^ 2) for i in every]
    core_pairs = [(i, i ^ 1) for i in every]
    along_pairs = [(i, (i + (-4 if i & 2 else 4)) % members) for i in every]
    along_core_pairs = [(i, (i + (-3 if i & 2 else 3)) % members) for i in every if i % 4 in (1, 2)]
    permute = lambda value, pairs: lax.ppermute(value, "pts", pairs)
    meet = lambda *values: lax.optimization_barrier(values)
    quads = members // 4
    reach = list(dict.fromkeys(step % quads for step in (0, 1, -1, 2, -2)))

    rhs_core = permute(rhs, core_pairs)
    panel, entry, *parts = up(
        members,
        2 * len(reach) * RANK,
        source_basis,
        leaf_transfer,
        mid_transfer,
        near_ids,
        near_count.reshape(1, B_DEV),
        rhs,
    )
    parts[CARRIER], down_basis, placed = down(
        reach, members, far_ids, target_basis, leaf_transfer, mid_transfer, far_coupling[0], parts[CARRIER]
    )
    across = [permute(part, across_pairs) for part in parts[:3]]
    others = [permute(panel, [(i, (i - 4 * step) % members) for i in every]) for step in reach[1:]]
    across[0], panel, others[0], others[1] = meet(across[0], panel, others[0], others[1])
    asked = ask(panel, others[0], others[1], rhs_core, down_basis)
    wish = wishes(asked, permute(asked, core_pairs))

    nears, along, across_core = [], [], []

    def pieces(k):
        return (parts[k], rhs_core, across[k], across_core[k], *along[k])

    for k in range(len(SLABS)):
        if k >= 2:
            nears.append(near(*SLABS[k - 2], entry, near_blocks, pieces(k - 2), nears[-1:]))
        picks = list(pack(wish, across[k], across_core[-1:] + nears[-1:] if k else others[2:]))
        along.append([permute(picks[0], along_pairs), permute(picks[1], along_core_pairs)])
        if k == 1:
            nearby = jnp.concatenate([each[:RANK] for each in (panel, *others)], axis=0)
            nearby, along[0][1] = meet(nearby, along[0][1])
            core_nearby = permute(nearby, core_pairs)
        if k >= 1:
            picks[2], along[k - 1][0] = meet(picks[2], along[k - 1][0])
        across_core.append(permute(picks[2], core_pairs))
        if k == 1:
            parts[3], along[0][1] = meet(parts[3], along[0][1])
            across.append(permute(parts[3], across_pairs))
        if k == 2:
            own_sum, partner_sum = couple(placed, across[CARRIER], nearby, core_nearby)
            partner_sum, along[1][1] = meet(partner_sum, along[1][1])
            sums = (own_sum, permute(partner_sum, across_pairs))
    nears.append(near(*SLABS[2], entry, near_blocks, pieces(2), nears[-1:]))
    product = finish(SLABS[:-1], sums, down_basis, nears)
    return last(*SLABS[-1], entry, near_blocks, sums, down_basis, pieces(3), product)


def solution(mesh):
    return jax.shard_map(
        on_device,
        mesh=mesh,
        in_specs=(
            P(("parts", "pts"), None),
            P(("parts", "pts"), None, None, None),
            P(("parts", "pts"), None),
            P(("parts", "pts")),
            P(("parts", "pts"), None, None),
            P(("parts", "pts"), None, None),
            P(("parts", "pts"), None, None),
            P(("parts", "pts"), None, None),
            P(("parts", "pts"), None, None, None),
            P(("parts", "pts"), None),
        ),
        out_specs=P(("parts", "pts"), None),
        check_vma=False,
    )
```

```python
import functools

import jax
import jax.numpy as jnp
from jax import lax
from jax.experimental import pallas as pl
from jax.experimental.pallas import tpu as pltpu
from jax.sharding import PartitionSpec as P

LEAF = 256
RANK = 64
B_DEV = 4
NEAR = 12
ROWS = B_DEV * LEAF
SLABS = ((0, 256), (256, 256), (512, 256), (768, 256))
CARRIER = 2
WISH = 16
OWN, CORE, ACROSS, ACROSS_CORE, ALONG, ALONG_CORE, ZERO = 0, 4, 8, 12, 14, 16, 18
HELD = 19
HELD_AT = (
    (ALONG, ALONG_CORE, OWN, CORE, ACROSS),
    (ALONG, CORE, OWN, ACROSS_CORE, ACROSS),
    (ACROSS, ACROSS_CORE, OWN, CORE, ALONG),
    (ACROSS, CORE, OWN, ALONG_CORE, ALONG),
)
MIB = 1024 * 1024
STEP = 0.4
UP_LIMIT = 58
BYTES = 1
XJOIN = 3
ZJ = 1.5
XC0 = 0
ANYWHERE = pl.BlockSpec(memory_space=pl.ANY)
VECTOR = pl.BlockSpec(memory_space=pltpu.VMEM)
SCALAR = pl.BlockSpec(memory_space=pltpu.SMEM)


def cost(microseconds):
    return pl.CostEstimate(flops=int(microseconds * 1.15e9), bytes_accessed=BYTES * MIB, transcendentals=0)


def split(value):
    high = value.astype(jnp.bfloat16)
    low = (value - high.astype(jnp.float32)).astype(jnp.bfloat16)
    return high, low


def dot(a, b):
    return jnp.dot(a, b, preferred_element_type=jnp.float32)


def dot_split(a, b):
    high, low = split(a)
    both = dot(jnp.concatenate([high, low], axis=0), b)
    return both[: a.shape[0]] + both[a.shape[0] :]


def first_two(named):
    first = jnp.where(named[0], 0, jnp.where(named[1], 1, jnp.where(named[2], 2, 3)))
    second = jnp.where(named[1] & (first < 1), 1, jnp.where(named[2] & (first < 2), 2, 3))
    return first, second


def places(members, position, numbers, counts):
    distance = (numbers >> 2) - position + 2
    distance = jnp.where(distance < 0, distance + members, distance)
    distance = jnp.where(distance >= members, distance - members, distance)
    base = jnp.full(numbers.shape, ZERO, jnp.int32)
    for d in range(5):
        at = jnp.int32(HELD_AT[0][d])
        for kind in range(1, 4):
            at = jnp.where(position & 3 == kind, HELD_AT[kind][d], at)
        base = jnp.where(distance == d, at, base)
    row = lax.broadcasted_iota(jnp.int32, (B_DEV, B_DEV), 0)
    column = lax.broadcasted_iota(jnp.int32, (B_DEV, B_DEV), 1)
    counts = jnp.max(jnp.where(row == column, counts, 0), axis=1, keepdims=True)
    live = lax.broadcasted_iota(jnp.int32, numbers.shape, 1) < counts
    base = jnp.where(live, base, ZERO)
    inner = numbers & 3
    picks = []
    for group in (ALONG, ALONG_CORE, ACROSS_CORE):
        named = []
        for box in range(B_DEV):
            here = jnp.where((base == group) & (inner == box), 1, 0)
            named.append(jnp.max(jnp.max(here, axis=1, keepdims=True), axis=0, keepdims=True) > 0)
        picks.append(first_two(named))
    return base, inner, picks


def up_kernel(members, *refs):
    given, rest = refs[:7], refs[7:]
    panel_ref, entry_ref, *parts = rest[: 1 + len(SLABS)]
    *kept, first_ref, sems = rest[1 + len(SLABS) :]
    pairs = list(zip(given[:5], kept))
    pairs += [
        (given[5].at[:, pl.ds(start, width)], part.at[pl.ds(0, ROWS)])
        for (start, width), part in zip(SLABS[1:], parts)
    ]
    pairs.append((given[6], first_ref))
    copies = [pltpu.make_async_copy(a, b, sems.at[i]) for i, (a, b) in enumerate(pairs)]
    for copy in copies:
        copy.start()
    source_ref, leaf_ref, mid_ref, ids_ref, count_ref = kept
    for copy in copies[:5]:
        copy.wait()
    base, inner, picks = places(members, lax.axis_index("pts"), ids_ref[...], count_ref[...])
    first = jnp.where(base == ALONG, picks[0][0], jnp.where(base == ALONG_CORE, picks[1][0], picks[2][0]))
    picked = jnp.where(inner == first, 0, 1)
    entry_ref[...] = base + jnp.where(base == ZERO, 0, jnp.where(base >= ACROSS_CORE, picked, inner))
    for k, name in enumerate(pick[n] for pick in picks for n in range(2)):
        panel_ref[pl.ds(RANK, WISH), pl.ds(k * 128, 128)] = jnp.broadcast_to(
            name.astype(jnp.float32), (WISH, 128)
        ).astype(jnp.bfloat16)
    panel_ref[pl.ds(RANK, WISH), pl.ds(6 * 128, 2 * 128)] = jnp.zeros((WISH, 2 * 128), jnp.bfloat16)
    ups = [dot_split(dot(mid_ref[box // 2], leaf_ref[box]), source_ref[box]) for box in range(B_DEV)]
    high, low = split(jnp.concatenate(ups, axis=1))
    both = jnp.concatenate([high, low], axis=0)
    for copy, (start, width), part in zip(copies[5:], SLABS[1:] + SLABS[:1], [*parts, first_ref]):
        copy.wait()
        sums = dot(both, part[pl.ds(0, ROWS)])
        panel_ref[pl.ds(0, RANK), pl.ds(start, width)] = (sums[:RANK] + sums[RANK:]).astype(jnp.bfloat16)


def up(members, carried, *given):
    columns = given[5].shape[1]
    shapes = [(ROWS, width) for _, width in SLABS]
    shapes[CARRIER] = (ROWS + RANK * -(-carried // shapes[CARRIER][1]), shapes[CARRIER][1])
    return pl.pallas_call(
        functools.partial(up_kernel, members),
        in_specs=[ANYWHERE] * len(given),
        out_shape=(
            jax.ShapeDtypeStruct((RANK + WISH, columns), jnp.bfloat16),
            jax.ShapeDtypeStruct((B_DEV, NEAR), jnp.int32),
            *[jax.ShapeDtypeStruct(shape, jnp.bfloat16) for shape in shapes[1:]],
        ),
        scratch_shapes=[pltpu.VMEM(a.shape, a.dtype) for a in (*given[:5], given[6])]
        + [pltpu.SemaphoreType.DMA((5 + len(SLABS),))],
        compiler_params=pltpu.CompilerParams(vmem_limit_bytes=UP_LIMIT * MIB),
        cost_estimate=cost(2),
        name="up",
    )(*given)


def down_kernel(reach, members, far_ref, target_ref, leaf_ref, mid_ref, coupling_ref, *rest):
    part_ref, down_ref, placed_ref, lines_ref, sem = rest[-5:]
    for box in range(B_DEV):
        chain = dot(mid_ref[box // 2], leaf_ref[box])
        high, low = split(dot_split(chain, target_ref[box]).T)
        down_ref[box] = jnp.concatenate([high, low, high], axis=1)
    position = lax.axis_index("pts")
    quad, side, core = position >> 2, (position >> 1) & 1, position & 1
    for half in range(2):
        blocks = []
        for other in range(2):
            for step in reach:
                held_quad = quad + step
                held_quad = jnp.where(held_quad >= members // 4, held_quad - members // 4, held_quad)
                group = held_quad * 4 + 2 * (side ^ half) + (core ^ other)
                block = jnp.zeros((RANK, RANK), jnp.float32)
                for f in range(coupling_ref.shape[0]):
                    block = jnp.where(far_ref[0, f] == group, coupling_ref[f].astype(jnp.float32), block)
                blocks.append(block)
        placed = jnp.concatenate(blocks, axis=1).astype(jnp.bfloat16)
        if half == 0:
            placed_ref[...] = placed
            continue
        width = part_ref.shape[1]
        for line, at in enumerate(range(0, placed.shape[1], width)):
            taken = placed[:, at : at + width]
            lines_ref[pl.ds(line * RANK, RANK), pl.ds(0, taken.shape[1])] = taken
        copy = pltpu.make_async_copy(lines_ref, part_ref.at[pl.ds(ROWS, lines_ref.shape[0])], sem)
        copy.start()
        copy.wait()


def down(reach, members, far_ids, target_basis, leaf_transfer, mid_transfer, coupling, part, *before):
    return pl.pallas_call(
        functools.partial(down_kernel, reach, members),
        in_specs=[SCALAR] + [VECTOR] * 4 + [ANYWHERE] + [VECTOR] * len(before),
        out_specs=(ANYWHERE, VECTOR, VECTOR),
        out_shape=(
            jax.ShapeDtypeStruct(part.shape, part.dtype),
            jax.ShapeDtypeStruct((B_DEV, LEAF, 3 * RANK), jnp.bfloat16),
            jax.ShapeDtypeStruct((RANK, 2 * len(reach) * RANK), jnp.bfloat16),
        ),
        scratch_shapes=[
            pltpu.VMEM((part.shape[0] - ROWS, part.shape[1]), part.dtype),
            pltpu.SemaphoreType.DMA,
        ],
        input_output_aliases={5: 0},
        compiler_params=pltpu.CompilerParams(vmem_limit_bytes=16 * MIB),
        cost_estimate=cost(1),
        name="down",
    )(far_ids, target_basis, leaf_transfer, mid_transfer, coupling, part, *before)


def ask_kernel(panel_ref, ahead_ref, behind_ref, *rest):
    asked_ref = rest[-1]
    forth = (lax.axis_index("pts") & 2) == 0
    wishes = (pl.ds(RANK, WISH), pl.ds(0, 6 * 128))
    ahead, behind = ahead_ref[wishes].astype(jnp.float32), behind_ref[wishes].astype(jnp.float32)
    asked_ref[pl.ds(0, WISH)] = jnp.where(forth, ahead, behind).astype(jnp.bfloat16)
    asked_ref[pl.ds(WISH, WISH)] = panel_ref[wishes]


def ask(panel, ahead, behind, *before):
    return pl.pallas_call(
        ask_kernel,
        in_specs=[VECTOR] * 3 + [ANYWHERE] * len(before),
        out_shape=jax.ShapeDtypeStruct((2 * WISH, 6 * 128), jnp.bfloat16),
        compiler_params=pltpu.CompilerParams(vmem_limit_bytes=8 * MIB),
        cost_estimate=cost(0.1),
        name="ask",
    )(panel, ahead, behind, *before)


def wishes_kernel(asked_ref, core_asked_ref, wish_ref):
    for name in range(6):
        ref = asked_ref if name < 2 else core_asked_ref
        value = ref[pl.ds(0 if name < 4 else WISH, WISH), pl.ds(name * 128, 128)]
        wish_ref[0, name] = jnp.max(value.astype(jnp.float32)).astype(jnp.int32)


def wishes(asked, core_asked):
    return pl.pallas_call(
        wishes_kernel,
        in_specs=[VECTOR] * 2,
        out_specs=SCALAR,
        out_shape=jax.ShapeDtypeStruct((1, 6), jnp.int32),
        compiler_params=pltpu.CompilerParams(vmem_limit_bytes=8 * MIB),
        cost_estimate=cost(0.1),
        name="wishes",
    )(asked, core_asked)


def join_kernel(*refs):
    refs[-1][...] = jnp.zeros_like(refs[-1])


def join(microseconds, *values):
    return pl.pallas_call(
        join_kernel,
        in_specs=[ANYWHERE] * len(values),
        out_shape=jax.ShapeDtypeStruct((8, 128), jnp.float32),
        compiler_params=pltpu.CompilerParams(vmem_limit_bytes=MIB),
        cost_estimate=cost(microseconds),
        name="join",
    )(*values)


def couple_kernel(own_ref, carrier_ref, core_ref, *rest):
    panels, (own_sum_ref, partner_sum_ref) = rest[:-2], rest[-2:]
    depth = own_ref.shape[1]
    lines = [core_ref[pl.ds(row, depth // 2)] for row in range(2 * LEAF, core_ref.shape[0], depth // 2)]
    table = [ref[pl.ds(0, RANK)] for ref in panels] + [jnp.concatenate(lines, axis=1)]
    table = jnp.concatenate(table, axis=0)
    lines = [carrier_ref[pl.ds(row, RANK)] for row in range(ROWS, carrier_ref.shape[0], RANK)]
    partner_sum = dot(jnp.concatenate(lines, axis=1)[:, :depth], table)
    partner_sum_ref[...] = partner_sum.astype(jnp.bfloat16)
    own_sum_ref[...] = dot(own_ref[...], table)


def couple(own, carrier, core, *panels):
    shape = (RANK, panels[0].shape[1])
    return pl.pallas_call(
        couple_kernel,
        out_shape=(jax.ShapeDtypeStruct(shape, jnp.float32), jax.ShapeDtypeStruct(shape, jnp.bfloat16)),
        compiler_params=pltpu.CompilerParams(vmem_limit_bytes=16 * MIB),
        cost_estimate=cost(0.1),
        name="couple",
    )(own, carrier, core, *panels)


def pick(wish_ref, at, arrived_ref, picked_ref):
    for k in range(2):
        rows = pl.ds(pl.multiple_of(wish_ref[0, at + k] * LEAF, LEAF), LEAF)
        picked_ref[pl.ds(k * LEAF, LEAF)] = arrived_ref[rows]


def pack_kernel(panels, wish_ref, arrived_ref, *rest):
    for at, picked_ref in enumerate(rest[-3:]):
        pick(wish_ref, 2 * at, arrived_ref, picked_ref)
    to = 2 * LEAF
    for at in range(0, rest[0].shape[1] if panels else 0, arrived_ref.shape[1]):
        for ref in rest[:panels]:
            rest[-1][pl.ds(to, RANK)] = ref[pl.ds(0, RANK), pl.ds(at, arrived_ref.shape[1])]
            to += RANK


def pack(wish, arrived, panels, before):
    width = arrived.shape[1]
    shape = jax.ShapeDtypeStruct((2 * LEAF, width), arrived.dtype)
    further = sum(RANK * panel.shape[1] // width for panel in panels)
    return pl.pallas_call(
        functools.partial(pack_kernel, len(panels)),
        in_specs=[SCALAR] + [VECTOR] * (1 + len(panels)) + [ANYWHERE] * len(before),
        out_shape=(shape, shape, jax.ShapeDtypeStruct((2 * LEAF + further, width), arrived.dtype)),
        compiler_params=pltpu.CompilerParams(vmem_limit_bytes=8 * MIB),
        cost_estimate=cost(0.02),
        name="pack",
    )(wish, arrived, *panels, *before)


def gather(start, width, held, pieces):
    own_ref, core_ref, across_ref, across_core_ref, along_ref, along_core_ref = pieces
    for at, boxes, taken in (
        (OWN, B_DEV, own_ref[pl.ds(0, ROWS)]),
        (CORE, B_DEV, core_ref[:, pl.ds(start, width)]),
        (ACROSS, B_DEV, across_ref[pl.ds(0, ROWS)]),
        (ACROSS_CORE, 2, across_core_ref[pl.ds(0, 2 * LEAF)]),
        (ALONG, 2, along_ref[...]),
        (ALONG_CORE, 2, along_core_ref[...]),
    ):
        held[pl.ds(at * LEAF, boxes * LEAF)] = taken
    held[pl.ds(ZERO * LEAF, LEAF)] = jnp.zeros((LEAF, width), jnp.bfloat16)


def operands(box, entry_ref, near_ref, held):
    left = [near_ref[box, n] for n in range(NEAR)]
    right = [held[pl.ds(pl.multiple_of(entry_ref[box, n] * LEAF, LEAF), LEAF)] for n in range(NEAR)]
    return left, right


def near_kernel(start, entry_ref, near_ref, *rest):
    pieces, (sum_ref, held) = rest[:6], rest[-2:]
    gather(start, sum_ref.shape[1], held, pieces)
    for box in range(B_DEV):
        left, right = operands(box, entry_ref, near_ref, held)
        sum_ref[pl.ds(box * LEAF, LEAF)] = dot(
            jnp.concatenate(left, axis=1), jnp.concatenate(right, axis=0)
        )


def near(start, width, entry, near_blocks, pieces, before):
    return pl.pallas_call(
        functools.partial(near_kernel, start),
        in_specs=[SCALAR] + [VECTOR] * (1 + len(pieces)) + [ANYWHERE] * len(before),
        out_specs=VECTOR,
        scratch_shapes=[pltpu.VMEM((HELD * LEAF, width), jnp.bfloat16)],
        out_shape=jax.ShapeDtypeStruct((ROWS, width), jnp.float32),
        compiler_params=pltpu.CompilerParams(vmem_limit_bytes=16 * MIB),
        cost_estimate=cost(STEP),
        name="near",
    )(entry, near_blocks, *pieces, *before)


def last_kernel(start, width, entry_ref, near_ref, own_sum_ref, partner_sum_ref, down_ref, *rest):
    pieces, (out_ref, held, made, sems) = rest[:6], rest[-4:]
    gather(start, width, held, pieces)
    taken = pl.ds(start, width)
    high, low = split(own_sum_ref[:, taken] + partner_sum_ref[:, taken].astype(jnp.float32))
    coupled = jnp.concatenate([high, high, low], axis=0)
    copies = []
    for box in range(B_DEV):
        left, right = operands(box, entry_ref, near_ref, held)
        rows = pl.ds(box * LEAF, LEAF)
        near_sum = dot(jnp.concatenate(left, axis=1), jnp.concatenate(right, axis=0))
        made[rows] = (near_sum + dot(down_ref[box], coupled)).astype(jnp.bfloat16)
        copy = pltpu.make_async_copy(made.at[rows], out_ref.at[rows, taken], sems.at[box])
        copy.start()
        copies.append(copy)
    for copy in copies:
        copy.wait()


def last(start, width, entry, near_blocks, sums, down_basis, pieces, mark, product):
    given = [entry, near_blocks, *sums, down_basis, *pieces, mark, product]
    return pl.pallas_call(
        functools.partial(last_kernel, start, width),
        in_specs=[SCALAR] + [VECTOR] * (len(given) - 3) + [ANYWHERE] * 2,
        out_specs=ANYWHERE,
        scratch_shapes=[
            pltpu.VMEM((HELD * LEAF, width), jnp.bfloat16),
            pltpu.VMEM((ROWS, width), jnp.bfloat16),
            pltpu.SemaphoreType.DMA((B_DEV,)),
        ],
        out_shape=jax.ShapeDtypeStruct(product.shape, product.dtype),
        input_output_aliases={len(given) - 1: 0},
        compiler_params=pltpu.CompilerParams(vmem_limit_bytes=16 * MIB),
        cost_estimate=cost(1),
        name="last",
    )(*given)


def finish_kernel(slabs, own_sum_ref, partner_sum_ref, down_ref, *rest):
    sum_refs = rest[: len(slabs)]
    out_ref, made, sems = rest[-3:]
    start, stop = slabs[0][0], slabs[-1][0] + slabs[-1][1]
    taken = pl.ds(start, stop - start)
    high, low = split(own_sum_ref[:, taken] + partner_sum_ref[:, taken].astype(jnp.float32))
    coupled = jnp.concatenate([high, high, low], axis=0)
    copies = []
    for box in range(B_DEV):
        rows = pl.ds(box * LEAF, LEAF)
        far = dot(down_ref[box], coupled)
        for (at, width), sum_ref in zip(slabs, sum_refs):
            columns = slice(at - start, at - start + width)
            made[rows, columns] = (far[:, columns] + sum_ref[rows]).astype(jnp.bfloat16)
        copy = pltpu.make_async_copy(made.at[rows], out_ref.at[rows, taken], sems.at[box])
        copy.start()
        copies.append(copy)
    for copy in copies:
        copy.wait()


def finish(slabs, sums, down_basis, nears):
    columns = sums[0].shape[1]
    given = [*sums, down_basis, *nears]
    return pl.pallas_call(
        functools.partial(finish_kernel, slabs),
        in_specs=[VECTOR] * len(given),
        out_specs=ANYWHERE,
        scratch_shapes=[
            pltpu.VMEM((ROWS, sum(width for _, width in slabs)), jnp.bfloat16),
            pltpu.SemaphoreType.DMA((B_DEV,)),
        ],
        out_shape=jax.ShapeDtypeStruct((ROWS, columns), jnp.bfloat16),
        compiler_params=pltpu.CompilerParams(vmem_limit_bytes=16 * MIB),
        cost_estimate=cost(STEP),
        name="finish",
    )(*given)


def on_device(
    rhs,
    near_blocks,
    near_ids,
    near_count,
    source_basis,
    target_basis,
    leaf_transfer,
    mid_transfer,
    far_coupling,
    far_ids,
):
    members = lax.axis_size("pts")
    every = range(members)
    across_pairs = [(i, i ^ 2) for i in every]
    core_pairs = [(i, i ^ 1) for i in every]
    along_pairs = [(i, (i + (-4 if i & 2 else 4)) % members) for i in every]
    along_core_pairs = [(i, (i + (-3 if i & 2 else 3)) % members) for i in every if i % 4 in (1, 2)]
    permute = lambda value, pairs: lax.ppermute(value, "pts", pairs)
    meet = lambda *values: lax.optimization_barrier(values)
    quads = members // 4
    reach = list(dict.fromkeys(step % quads for step in (0, 1, -1, 2, -2)))

    rhs_core = permute(rhs, core_pairs)
    first = rhs[:, : SLABS[0][1]]
    panel, entry, *parts = up(
        members,
        2 * len(reach) * RANK,
        source_basis,
        leaf_transfer,
        mid_transfer,
        near_ids,
        near_count.reshape(1, B_DEV),
        rhs,
        first,
    )
    parts = [first, *parts]
    parts[CARRIER], down_basis, placed = down(
        reach, members, far_ids, target_basis, leaf_transfer, mid_transfer, far_coupling[0], parts[CARRIER], panel
    )
    across = [permute(part, across_pairs) for part in parts[:3]]
    others = [permute(panel, [(i, (i - 4 * step) % members) for i in every]) for step in reach[1:]]
    across[0], panel, others[0], others[1] = meet(across[0], panel, others[0], others[1])
    asked = ask(panel, others[0], others[1], rhs_core, down_basis)
    wish = wishes(asked, permute(asked, core_pairs))

    nears, along, across_core = [], [], []

    def pieces(k):
        return (parts[k], rhs_core, across[k], across_core[k], *along[k])

    for k in range(len(SLABS)):
        if k >= 2:
            nears.append(near(*SLABS[k - 2], entry, near_blocks, pieces(k - 2), nears[-1:] + [join(ZJ, *along[k - 2])]))
        panels = [panel, *others] if k == 0 else []
        before = nears[-1:] + (across_core[:1] if k == 1 and XC0 else [])
        if k == 1 and XJOIN:
            before.append(join(XJOIN, across[1]))
        picks = list(pack(wish, across[k], panels, before))
        along.append([permute(picks[0], along_pairs), permute(picks[1], along_core_pairs)])
        if k >= 1:
            picks[2], along[k - 1][0] = meet(picks[2], along[k - 1][0])
        across_core.append(permute(picks[2], core_pairs))
        if k == 1:
            parts[3], along[0][1] = meet(parts[3], along[0][1])
            across.append(permute(parts[3], across_pairs))
    own_sum, partner_sum = couple(placed, across[CARRIER], across_core[0], panel, *others)
    sums = (own_sum, permute(partner_sum, across_pairs))
    nears.append(near(*SLABS[2], entry, near_blocks, pieces(2), nears[-1:] + [join(ZJ, *along[2])]))
    product = finish(SLABS[:-1], sums, down_basis, nears)
    return last(*SLABS[-1], entry, near_blocks, sums, down_basis, pieces(3), join(ZJ, *along[3]), product)


def solution(mesh):
    return jax.shard_map(
        on_device,
        mesh=mesh,
        in_specs=(
            P(("parts", "pts"), None),
            P(("parts", "pts"), None, None, None),
            P(("parts", "pts"), None),
            P(("parts", "pts")),
            P(("parts", "pts"), None, None),
            P(("parts", "pts"), None, None),
            P(("parts", "pts"), None, None),
            P(("parts", "pts"), None, None),
            P(("parts", "pts"), None, None, None),
            P(("parts", "pts"), None),
        ),
        out_specs=P(("parts", "pts"), None),
        check_vma=False,
    )
```

```python
import functools

import jax
import jax.numpy as jnp
from jax import lax
from jax.experimental import pallas as pl
from jax.experimental.pallas import tpu as pltpu
from jax.sharding import PartitionSpec as P

LEAF = 256
RANK = 64
B_DEV = 4
NEAR = 12
ROWS = B_DEV * LEAF
SLABS = ((0, 256), (256, 256), (512, 256), (768, 256))
CARRIER = 2
WISH = 16
OWN, CORE, ACROSS, ACROSS_CORE, ALONG, ALONG_CORE, ZERO = 0, 4, 8, 12, 14, 16, 18
HELD = 19
HELD_AT = (
    (ALONG, ALONG_CORE, OWN, CORE, ACROSS),
    (ALONG, CORE, OWN, ACROSS_CORE, ACROSS),
    (ACROSS, ACROSS_CORE, OWN, CORE, ALONG),
    (ACROSS, CORE, OWN, ALONG_CORE, ALONG),
)
MIB = 1024 * 1024
UP_LIMIT = 58
BYTES = 1
XJ = (0, 3, 0, 0)
ZJ = (1.5, 1.5, 1.5, 1.5)
XC = (0, 0, 0)
MC = (1, 1, 1)
M3 = 1
PK = 0
COSTS = (2, 1, 0.4, 0.4, 1, 0.02, 0.1)
ANYWHERE = pl.BlockSpec(memory_space=pl.ANY)
VECTOR = pl.BlockSpec(memory_space=pltpu.VMEM)
SCALAR = pl.BlockSpec(memory_space=pltpu.SMEM)


def cost(microseconds):
    return pl.CostEstimate(flops=int(microseconds * 1.15e9), bytes_accessed=BYTES * MIB, transcendentals=0)


def split(value):
    high = value.astype(jnp.bfloat16)
    low = (value - high.astype(jnp.float32)).astype(jnp.bfloat16)
    return high, low


def dot(a, b):
    return jnp.dot(a, b, preferred_element_type=jnp.float32)


def dot_split(a, b):
    high, low = split(a)
    both = dot(jnp.concatenate([high, low], axis=0), b)
    return both[: a.shape[0]] + both[a.shape[0] :]


def first_two(named):
    first = jnp.where(named[0], 0, jnp.where(named[1], 1, jnp.where(named[2], 2, 3)))
    second = jnp.where(named[1] & (first < 1), 1, jnp.where(named[2] & (first < 2), 2, 3))
    return first, second


def places(members, position, numbers, counts):
    distance = (numbers >> 2) - position + 2
    distance = jnp.where(distance < 0, distance + members, distance)
    distance = jnp.where(distance >= members, distance - members, distance)
    base = jnp.full(numbers.shape, ZERO, jnp.int32)
    for d in range(5):
        at = jnp.int32(HELD_AT[0][d])
        for kind in range(1, 4):
            at = jnp.where(position & 3 == kind, HELD_AT[kind][d], at)
        base = jnp.where(distance == d, at, base)
    row = lax.broadcasted_iota(jnp.int32, (B_DEV, B_DEV), 0)
    column = lax.broadcasted_iota(jnp.int32, (B_DEV, B_DEV), 1)
    counts = jnp.max(jnp.where(row == column, counts, 0), axis=1, keepdims=True)
    live = lax.broadcasted_iota(jnp.int32, numbers.shape, 1) < counts
    base = jnp.where(live, base, ZERO)
    inner = numbers & 3
    picks = []
    for group in (ALONG, ALONG_CORE, ACROSS_CORE):
        named = []
        for box in range(B_DEV):
            here = jnp.where((base == group) & (inner == box), 1, 0)
            named.append(jnp.max(jnp.max(here, axis=1, keepdims=True), axis=0, keepdims=True) > 0)
        picks.append(first_two(named))
    return base, inner, picks


def up_kernel(members, *refs):
    given, rest = refs[:7], refs[7:]
    panel_ref, entry_ref, *parts = rest[: 1 + len(SLABS)]
    *kept, first_ref, sems = rest[1 + len(SLABS) :]
    pairs = list(zip(given[:5], kept))
    pairs += [
        (given[5].at[:, pl.ds(start, width)], part.at[pl.ds(0, ROWS)])
        for (start, width), part in zip(SLABS[1:], parts)
    ]
    pairs.append((given[6], first_ref))
    copies = [pltpu.make_async_copy(a, b, sems.at[i]) for i, (a, b) in enumerate(pairs)]
    for copy in copies:
        copy.start()
    source_ref, leaf_ref, mid_ref, ids_ref, count_ref = kept
    for copy in copies[:5]:
        copy.wait()
    base, inner, picks = places(members, lax.axis_index("pts"), ids_ref[...], count_ref[...])
    first = jnp.where(base == ALONG, picks[0][0], jnp.where(base == ALONG_CORE, picks[1][0], picks[2][0]))
    picked = jnp.where(inner == first, 0, 1)
    entry_ref[...] = base + jnp.where(base == ZERO, 0, jnp.where(base >= ACROSS_CORE, picked, inner))
    for k, name in enumerate(pick[n] for pick in picks for n in range(2)):
        panel_ref[pl.ds(RANK, WISH), pl.ds(k * 128, 128)] = jnp.broadcast_to(
            name.astype(jnp.float32), (WISH, 128)
        ).astype(jnp.bfloat16)
    panel_ref[pl.ds(RANK, WISH), pl.ds(6 * 128, 2 * 128)] = jnp.zeros((WISH, 2 * 128), jnp.bfloat16)
    ups = [dot_split(dot(mid_ref[box // 2], leaf_ref[box]), source_ref[box]) for box in range(B_DEV)]
    high, low = split(jnp.concatenate(ups, axis=1))
    both = jnp.concatenate([high, low], axis=0)
    for copy, (start, width), part in zip(copies[5:], SLABS[1:] + SLABS[:1], [*parts, first_ref]):
        copy.wait()
        sums = dot(both, part[pl.ds(0, ROWS)])
        panel_ref[pl.ds(0, RANK), pl.ds(start, width)] = (sums[:RANK] + sums[RANK:]).astype(jnp.bfloat16)


def up(members, carried, *given):
    columns = given[5].shape[1]
    shapes = [(ROWS, width) for _, width in SLABS]
    shapes[CARRIER] = (ROWS + RANK * -(-carried // shapes[CARRIER][1]), shapes[CARRIER][1])
    return pl.pallas_call(
        functools.partial(up_kernel, members),
        in_specs=[ANYWHERE] * len(given),
        out_shape=(
            jax.ShapeDtypeStruct((RANK + WISH, columns), jnp.bfloat16),
            jax.ShapeDtypeStruct((B_DEV, NEAR), jnp.int32),
            *[jax.ShapeDtypeStruct(shape, jnp.bfloat16) for shape in shapes[1:]],
        ),
        scratch_shapes=[pltpu.VMEM(a.shape, a.dtype) for a in (*given[:5], given[6])]
        + [pltpu.SemaphoreType.DMA((5 + len(SLABS),))],
        compiler_params=pltpu.CompilerParams(vmem_limit_bytes=UP_LIMIT * MIB),
        cost_estimate=cost(COSTS[0]),
        name="up",
    )(*given)


def down_kernel(reach, members, far_ref, target_ref, leaf_ref, mid_ref, coupling_ref, *rest):
    part_ref, down_ref, placed_ref, lines_ref, sem = rest[-5:]
    for box in range(B_DEV):
        chain = dot(mid_ref[box // 2], leaf_ref[box])
        high, low = split(dot_split(chain, target_ref[box]).T)
        down_ref[box] = jnp.concatenate([high, low, high], axis=1)
    position = lax.axis_index("pts")
    quad, side, core = position >> 2, (position >> 1) & 1, position & 1
    for half in range(2):
        blocks = []
        for other in range(2):
            for step in reach:
                held_quad = quad + step
                held_quad = jnp.where(held_quad >= members // 4, held_quad - members // 4, held_quad)
                group = held_quad * 4 + 2 * (side ^ half) + (core ^ other)
                block = jnp.zeros((RANK, RANK), jnp.float32)
                for f in range(coupling_ref.shape[0]):
                    block = jnp.where(far_ref[0, f] == group, coupling_ref[f].astype(jnp.float32), block)
                blocks.append(block)
        placed = jnp.concatenate(blocks, axis=1).astype(jnp.bfloat16)
        if half == 0:
            placed_ref[...] = placed
            continue
        width = part_ref.shape[1]
        for line, at in enumerate(range(0, placed.shape[1], width)):
            taken = placed[:, at : at + width]
            lines_ref[pl.ds(line * RANK, RANK), pl.ds(0, taken.shape[1])] = taken
        copy = pltpu.make_async_copy(lines_ref, part_ref.at[pl.ds(ROWS, lines_ref.shape[0])], sem)
        copy.start()
        copy.wait()


def down(reach, members, far_ids, target_basis, leaf_transfer, mid_transfer, coupling, part, *before):
    return pl.pallas_call(
        functools.partial(down_kernel, reach, members),
        in_specs=[SCALAR] + [VECTOR] * 4 + [ANYWHERE] + [VECTOR] * len(before),
        out_specs=(ANYWHERE, VECTOR, VECTOR),
        out_shape=(
            jax.ShapeDtypeStruct(part.shape, part.dtype),
            jax.ShapeDtypeStruct((B_DEV, LEAF, 3 * RANK), jnp.bfloat16),
            jax.ShapeDtypeStruct((RANK, 2 * len(reach) * RANK), jnp.bfloat16),
        ),
        scratch_shapes=[
            pltpu.VMEM((part.shape[0] - ROWS, part.shape[1]), part.dtype),
            pltpu.SemaphoreType.DMA,
        ],
        input_output_aliases={5: 0},
        compiler_params=pltpu.CompilerParams(vmem_limit_bytes=16 * MIB),
        cost_estimate=cost(COSTS[1]),
        name="down",
    )(far_ids, target_basis, leaf_transfer, mid_transfer, coupling, part, *before)


def ask_kernel(panel_ref, ahead_ref, behind_ref, *rest):
    asked_ref = rest[-1]
    forth = (lax.axis_index("pts") & 2) == 0
    wishes = (pl.ds(RANK, WISH), pl.ds(0, 6 * 128))
    ahead, behind = ahead_ref[wishes].astype(jnp.float32), behind_ref[wishes].astype(jnp.float32)
    asked_ref[pl.ds(0, WISH)] = jnp.where(forth, ahead, behind).astype(jnp.bfloat16)
    asked_ref[pl.ds(WISH, WISH)] = panel_ref[wishes]


def ask(panel, ahead, behind, *before):
    return pl.pallas_call(
        ask_kernel,
        in_specs=[VECTOR] * 3 + [ANYWHERE] * len(before),
        out_shape=jax.ShapeDtypeStruct((2 * WISH, 6 * 128), jnp.bfloat16),
        compiler_params=pltpu.CompilerParams(vmem_limit_bytes=8 * MIB),
        cost_estimate=cost(0.1),
        name="ask",
    )(panel, ahead, behind, *before)


def wishes_kernel(asked_ref, core_asked_ref, wish_ref):
    for name in range(6):
        ref = asked_ref if name < 2 else core_asked_ref
        value = ref[pl.ds(0 if name < 4 else WISH, WISH), pl.ds(name * 128, 128)]
        wish_ref[0, name] = jnp.max(value.astype(jnp.float32)).astype(jnp.int32)


def wishes(asked, core_asked):
    return pl.pallas_call(
        wishes_kernel,
        in_specs=[VECTOR] * 2,
        out_specs=SCALAR,
        out_shape=jax.ShapeDtypeStruct((1, 6), jnp.int32),
        compiler_params=pltpu.CompilerParams(vmem_limit_bytes=8 * MIB),
        cost_estimate=cost(0.1),
        name="wishes",
    )(asked, core_asked)


def join_kernel(*refs):
    refs[-1][...] = jnp.zeros_like(refs[-1])


def join(microseconds, *values):
    return pl.pallas_call(
        join_kernel,
        in_specs=[ANYWHERE] * len(values),
        out_shape=jax.ShapeDtypeStruct((8, 128), jnp.float32),
        compiler_params=pltpu.CompilerParams(vmem_limit_bytes=MIB),
        cost_estimate=cost(microseconds),
        name="join",
    )(*values)


def couple_kernel(own_ref, carrier_ref, core_ref, *rest):
    panels, (own_sum_ref, partner_sum_ref) = rest[:-2], rest[-2:]
    depth = own_ref.shape[1]
    lines = [core_ref[pl.ds(row, depth // 2)] for row in range(2 * LEAF, core_ref.shape[0], depth // 2)]
    table = [ref[pl.ds(0, RANK)] for ref in panels] + [jnp.concatenate(lines, axis=1)]
    table = jnp.concatenate(table, axis=0)
    lines = [carrier_ref[pl.ds(row, RANK)] for row in range(ROWS, carrier_ref.shape[0], RANK)]
    partner_sum = dot(jnp.concatenate(lines, axis=1)[:, :depth], table)
    partner_sum_ref[...] = partner_sum.astype(jnp.bfloat16)
    own_sum_ref[...] = dot(own_ref[...], table)


def couple(own, carrier, core, *panels):
    shape = (RANK, panels[0].shape[1])
    return pl.pallas_call(
        couple_kernel,
        out_shape=(jax.ShapeDtypeStruct(shape, jnp.float32), jax.ShapeDtypeStruct(shape, jnp.bfloat16)),
        compiler_params=pltpu.CompilerParams(vmem_limit_bytes=16 * MIB),
        cost_estimate=cost(COSTS[6]),
        name="couple",
    )(own, carrier, core, *panels)


def pick(wish_ref, at, arrived_ref, picked_ref):
    for k in range(2):
        rows = pl.ds(pl.multiple_of(wish_ref[0, at + k] * LEAF, LEAF), LEAF)
        picked_ref[pl.ds(k * LEAF, LEAF)] = arrived_ref[rows]


def pack_kernel(panels, wish_ref, arrived_ref, *rest):
    for at, picked_ref in enumerate(rest[-3:]):
        pick(wish_ref, 2 * at, arrived_ref, picked_ref)
    to = 2 * LEAF
    for at in range(0, rest[0].shape[1] if panels else 0, arrived_ref.shape[1]):
        for ref in rest[:panels]:
            rest[-1][pl.ds(to, RANK)] = ref[pl.ds(0, RANK), pl.ds(at, arrived_ref.shape[1])]
            to += RANK


def pack(wish, arrived, panels, before):
    width = arrived.shape[1]
    shape = jax.ShapeDtypeStruct((2 * LEAF, width), arrived.dtype)
    further = sum(RANK * panel.shape[1] // width for panel in panels)
    return pl.pallas_call(
        functools.partial(pack_kernel, len(panels)),
        in_specs=[SCALAR] + [VECTOR] * (1 + len(panels)) + [ANYWHERE] * len(before),
        out_shape=(shape, shape, jax.ShapeDtypeStruct((2 * LEAF + further, width), arrived.dtype)),
        compiler_params=pltpu.CompilerParams(vmem_limit_bytes=8 * MIB),
        cost_estimate=cost(COSTS[5]),
        name="pack",
    )(wish, arrived, *panels, *before)


def gather(start, width, held, pieces):
    own_ref, core_ref, across_ref, across_core_ref, along_ref, along_core_ref = pieces
    for at, boxes, taken in (
        (OWN, B_DEV, own_ref[pl.ds(0, ROWS)]),
        (CORE, B_DEV, core_ref[:, pl.ds(start, width)]),
        (ACROSS, B_DEV, across_ref[pl.ds(0, ROWS)]),
        (ACROSS_CORE, 2, across_core_ref[pl.ds(0, 2 * LEAF)]),
        (ALONG, 2, along_ref[...]),
        (ALONG_CORE, 2, along_core_ref[...]),
    ):
        held[pl.ds(at * LEAF, boxes * LEAF)] = taken
    held[pl.ds(ZERO * LEAF, LEAF)] = jnp.zeros((LEAF, width), jnp.bfloat16)


def operands(box, entry_ref, near_ref, held):
    left = [near_ref[box, n] for n in range(NEAR)]
    right = [held[pl.ds(pl.multiple_of(entry_ref[box, n] * LEAF, LEAF), LEAF)] for n in range(NEAR)]
    return left, right


def near_kernel(start, entry_ref, near_ref, *rest):
    pieces, (sum_ref, held) = rest[:6], rest[-2:]
    gather(start, sum_ref.shape[1], held, pieces)
    for box in range(B_DEV):
        left, right = operands(box, entry_ref, near_ref, held)
        sum_ref[pl.ds(box * LEAF, LEAF)] = dot(
            jnp.concatenate(left, axis=1), jnp.concatenate(right, axis=0)
        )


def near(start, width, entry, near_blocks, pieces, before):
    return pl.pallas_call(
        functools.partial(near_kernel, start),
        in_specs=[SCALAR] + [VECTOR] * (1 + len(pieces)) + [ANYWHERE] * len(before),
        out_specs=VECTOR,
        scratch_shapes=[pltpu.VMEM((HELD * LEAF, width), jnp.bfloat16)],
        out_shape=jax.ShapeDtypeStruct((ROWS, width), jnp.float32),
        compiler_params=pltpu.CompilerParams(vmem_limit_bytes=16 * MIB),
        cost_estimate=cost(COSTS[2]),
        name="near",
    )(entry, near_blocks, *pieces, *before)


def last_kernel(start, width, entry_ref, near_ref, own_sum_ref, partner_sum_ref, down_ref, *rest):
    pieces, (out_ref, held, made, sems) = rest[:6], rest[-4:]
    gather(start, width, held, pieces)
    taken = pl.ds(start, width)
    high, low = split(own_sum_ref[:, taken] + partner_sum_ref[:, taken].astype(jnp.float32))
    coupled = jnp.concatenate([high, high, low], axis=0)
    copies = []
    for box in range(B_DEV):
        left, right = operands(box, entry_ref, near_ref, held)
        rows = pl.ds(box * LEAF, LEAF)
        near_sum = dot(jnp.concatenate(left, axis=1), jnp.concatenate(right, axis=0))
        made[rows] = (near_sum + dot(down_ref[box], coupled)).astype(jnp.bfloat16)
        copy = pltpu.make_async_copy(made.at[rows], out_ref.at[rows, taken], sems.at[box])
        copy.start()
        copies.append(copy)
    for copy in copies:
        copy.wait()


def last(start, width, entry, near_blocks, sums, down_basis, pieces, mark, product):
    given = [entry, near_blocks, *sums, down_basis, *pieces, mark, product]
    return pl.pallas_call(
        functools.partial(last_kernel, start, width),
        in_specs=[SCALAR] + [VECTOR] * (len(given) - 3) + [ANYWHERE] * 2,
        out_specs=ANYWHERE,
        scratch_shapes=[
            pltpu.VMEM((HELD * LEAF, width), jnp.bfloat16),
            pltpu.VMEM((ROWS, width), jnp.bfloat16),
            pltpu.SemaphoreType.DMA((B_DEV,)),
        ],
        out_shape=jax.ShapeDtypeStruct(product.shape, product.dtype),
        input_output_aliases={len(given) - 1: 0},
        compiler_params=pltpu.CompilerParams(vmem_limit_bytes=16 * MIB),
        cost_estimate=cost(COSTS[4]),
        name="last",
    )(*given)


def finish_kernel(slabs, own_sum_ref, partner_sum_ref, down_ref, *rest):
    sum_refs = rest[: len(slabs)]
    out_ref, made, sems = rest[-3:]
    start, stop = slabs[0][0], slabs[-1][0] + slabs[-1][1]
    taken = pl.ds(start, stop - start)
    high, low = split(own_sum_ref[:, taken] + partner_sum_ref[:, taken].astype(jnp.float32))
    coupled = jnp.concatenate([high, high, low], axis=0)
    copies = []
    for box in range(B_DEV):
        rows = pl.ds(box * LEAF, LEAF)
        far = dot(down_ref[box], coupled)
        for (at, width), sum_ref in zip(slabs, sum_refs):
            columns = slice(at - start, at - start + width)
            made[rows, columns] = (far[:, columns] + sum_ref[rows]).astype(jnp.bfloat16)
        copy = pltpu.make_async_copy(made.at[rows], out_ref.at[rows, taken], sems.at[box])
        copy.start()
        copies.append(copy)
    for copy in copies:
        copy.wait()


def finish(slabs, sums, down_basis, nears):
    columns = sums[0].shape[1]
    given = [*sums, down_basis, *nears]
    return pl.pallas_call(
        functools.partial(finish_kernel, slabs),
        in_specs=[VECTOR] * len(given),
        out_specs=ANYWHERE,
        scratch_shapes=[
            pltpu.VMEM((ROWS, sum(width for _, width in slabs)), jnp.bfloat16),
            pltpu.SemaphoreType.DMA((B_DEV,)),
        ],
        out_shape=jax.ShapeDtypeStruct((ROWS, columns), jnp.bfloat16),
        compiler_params=pltpu.CompilerParams(vmem_limit_bytes=16 * MIB),
        cost_estimate=cost(COSTS[3]),
        name="finish",
    )(*given)


def on_device(
    rhs,
    near_blocks,
    near_ids,
    near_count,
    source_basis,
    target_basis,
    leaf_transfer,
    mid_transfer,
    far_coupling,
    far_ids,
):
    members = lax.axis_size("pts")
    every = range(members)
    across_pairs = [(i, i ^ 2) for i in every]
    core_pairs = [(i, i ^ 1) for i in every]
    along_pairs = [(i, (i + (-4 if i & 2 else 4)) % members) for i in every]
    along_core_pairs = [(i, (i + (-3 if i & 2 else 3)) % members) for i in every if i % 4 in (1, 2)]
    permute = lambda value, pairs: lax.ppermute(value, "pts", pairs)
    meet = lambda *values: lax.optimization_barrier(values)
    quads = members // 4
    reach = list(dict.fromkeys(step % quads for step in (0, 1, -1, 2, -2)))

    rhs_core = permute(rhs, core_pairs)
    first = rhs[:, : SLABS[0][1]]
    panel, entry, *parts = up(
        members,
        2 * len(reach) * RANK,
        source_basis,
        leaf_transfer,
        mid_transfer,
        near_ids,
        near_count.reshape(1, B_DEV),
        rhs,
        first,
    )
    parts = [first, *parts]
    parts[CARRIER], down_basis, placed = down(
        reach, members, far_ids, target_basis, leaf_transfer, mid_transfer, far_coupling[0], parts[CARRIER], panel
    )
    across = [permute(part, across_pairs) for part in parts[:3]]
    others = [permute(panel, [(i, (i - 4 * step) % members) for i in every]) for step in reach[1:]]
    across[0], panel, others[0], others[1] = meet(across[0], panel, others[0], others[1])
    asked = ask(panel, others[0], others[1], rhs_core, down_basis)
    wish = wishes(asked, permute(asked, core_pairs))

    nears, along, across_core = [], [], []

    def marked(microseconds, *values):
        return [join(microseconds, *values)] if microseconds else []

    def pieces(k):
        return (parts[k], rhs_core, across[k], across_core[k], *along[k])

    for k in range(len(SLABS)):
        if k >= 2:
            nears.append(near(*SLABS[k - 2], entry, near_blocks, pieces(k - 2), nears[-1:] + marked(ZJ[k - 2], *along[k - 2])))
        panels = [panel, *others] if k == PK else []
        before = nears[-1:] + marked(XJ[k], across[k])
        if k and XC[k - 1]:
            before.append(across_core[k - 1])
        picks = list(pack(wish, across[k], panels, before))
        along.append([permute(picks[0], along_pairs), permute(picks[1], along_core_pairs)])
        if k and MC[k - 1]:
            picks[2], along[k - 1][0] = meet(picks[2], along[k - 1][0])
        across_core.append(permute(picks[2], core_pairs))
        if k == 1:
            if M3:
                parts[3], along[0][M3 - 1] = meet(parts[3], along[0][M3 - 1])
            across.append(permute(parts[3], across_pairs))
    own_sum, partner_sum = couple(placed, across[CARRIER], across_core[PK], panel, *others)
    sums = (own_sum, permute(partner_sum, across_pairs))
    nears.append(near(*SLABS[2], entry, near_blocks, pieces(2), nears[-1:] + marked(ZJ[2], *along[2])))
    product = finish(SLABS[:-1], sums, down_basis, nears)
    return last(*SLABS[-1], entry, near_blocks, sums, down_basis, pieces(3), join(ZJ[3], *along[3]), product)


def solution(mesh):
    return jax.shard_map(
        on_device,
        mesh=mesh,
        in_specs=(
            P(("parts", "pts"), None),
            P(("parts", "pts"), None, None, None),
            P(("parts", "pts"), None),
            P(("parts", "pts")),
            P(("parts", "pts"), None, None),
            P(("parts", "pts"), None, None),
            P(("parts", "pts"), None, None),
            P(("parts", "pts"), None, None),
            P(("parts", "pts"), None, None, None),
            P(("parts", "pts"), None),
        ),
        out_specs=P(("parts", "pts"), None),
        check_vma=False,
    )
```

```python
import functools

import jax
import jax.numpy as jnp
from jax import lax
from jax.experimental import pallas as pl
from jax.experimental.pallas import tpu as pltpu
from jax.sharding import PartitionSpec as P

LEAF = 256
RANK = 64
B_DEV = 4
NEAR = 12
ROWS = B_DEV * LEAF
SLABS = ((0, 256), (256, 256), (512, 256), (768, 256))
CARRIER = 2
WISH = 16
OWN, CORE, ACROSS, ACROSS_CORE, ALONG, ALONG_CORE, ZERO = 0, 4, 8, 12, 14, 16, 18
HELD = 19
HELD_AT = (
    (ALONG, ALONG_CORE, OWN, CORE, ACROSS),
    (ALONG, CORE, OWN, ACROSS_CORE, ACROSS),
    (ACROSS, ACROSS_CORE, OWN, CORE, ALONG),
    (ACROSS, CORE, OWN, ALONG_CORE, ALONG),
)
MIB = 1024 * 1024
UP_LIMIT = 58
BYTES = 1
XJ = (0, 3, 0, 0)
ZJ = (1.5, 1.5, 1.5, 1.5)
XC = (0, 0, 0)
MC = (1, 1, 1)
M3 = 1
PK = 0
COSTS = (2, 1, 0.4, 0.4, 1, 0.02, 0.1)
ANYWHERE = pl.BlockSpec(memory_space=pl.ANY)
VECTOR = pl.BlockSpec(memory_space=pltpu.VMEM)
SCALAR = pl.BlockSpec(memory_space=pltpu.SMEM)


def cost(microseconds):
    return pl.CostEstimate(flops=int(microseconds * 1.15e9), bytes_accessed=BYTES * MIB, transcendentals=0)


def split(value):
    high = value.astype(jnp.bfloat16)
    low = (value - high.astype(jnp.float32)).astype(jnp.bfloat16)
    return high, low


def dot(a, b):
    return jnp.dot(a, b, preferred_element_type=jnp.float32)


def dot_split(a, b):
    high, low = split(a)
    both = dot(jnp.concatenate([high, low], axis=0), b)
    return both[: a.shape[0]] + both[a.shape[0] :]


def first_two(named):
    first = jnp.where(named[0], 0, jnp.where(named[1], 1, jnp.where(named[2], 2, 3)))
    second = jnp.where(named[1] & (first < 1), 1, jnp.where(named[2] & (first < 2), 2, 3))
    return first, second


def places(members, position, numbers, counts):
    distance = (numbers >> 2) - position + 2
    distance = jnp.where(distance < 0, distance + members, distance)
    distance = jnp.where(distance >= members, distance - members, distance)
    base = jnp.full(numbers.shape, ZERO, jnp.int32)
    for d in range(5):
        at = jnp.int32(HELD_AT[0][d])
        for kind in range(1, 4):
            at = jnp.where(position & 3 == kind, HELD_AT[kind][d], at)
        base = jnp.where(distance == d, at, base)
    row = lax.broadcasted_iota(jnp.int32, (B_DEV, B_DEV), 0)
    column = lax.broadcasted_iota(jnp.int32, (B_DEV, B_DEV), 1)
    counts = jnp.max(jnp.where(row == column, counts, 0), axis=1, keepdims=True)
    live = lax.broadcasted_iota(jnp.int32, numbers.shape, 1) < counts
    base = jnp.where(live, base, ZERO)
    inner = numbers & 3
    picks = []
    for group in (ALONG, ALONG_CORE, ACROSS_CORE):
        named = []
        for box in range(B_DEV):
            here = jnp.where((base == group) & (inner == box), 1, 0)
            named.append(jnp.max(jnp.max(here, axis=1, keepdims=True), axis=0, keepdims=True) > 0)
        picks.append(first_two(named))
    return base, inner, picks


def up_kernel(members, *refs):
    given, rest = refs[:7], refs[7:]
    panel_ref, plain_ref, entry_ref, *parts = rest[: 2 + len(SLABS)]
    *kept, first_ref, sems = rest[2 + len(SLABS) :]
    pairs = list(zip(given[:5], kept))
    pairs += [
        (given[5].at[:, pl.ds(start, width)], part.at[pl.ds(0, ROWS)])
        for (start, width), part in zip(SLABS[1:], parts)
    ]
    pairs.append((given[6], first_ref))
    copies = [pltpu.make_async_copy(a, b, sems.at[i]) for i, (a, b) in enumerate(pairs)]
    for copy in copies:
        copy.start()
    source_ref, leaf_ref, mid_ref, ids_ref, count_ref = kept
    for copy in copies[:5]:
        copy.wait()
    base, inner, picks = places(members, lax.axis_index("pts"), ids_ref[...], count_ref[...])
    first = jnp.where(base == ALONG, picks[0][0], jnp.where(base == ALONG_CORE, picks[1][0], picks[2][0]))
    picked = jnp.where(inner == first, 0, 1)
    entry_ref[...] = base + jnp.where(base == ZERO, 0, jnp.where(base >= ACROSS_CORE, picked, inner))
    for k, name in enumerate(pick[n] for pick in picks for n in range(2)):
        panel_ref[pl.ds(RANK, WISH), pl.ds(k * 128, 128)] = jnp.broadcast_to(
            name.astype(jnp.float32), (WISH, 128)
        ).astype(jnp.bfloat16)
    panel_ref[pl.ds(RANK, WISH), pl.ds(6 * 128, 2 * 128)] = jnp.zeros((WISH, 2 * 128), jnp.bfloat16)
    ups = [dot_split(dot(mid_ref[box // 2], leaf_ref[box]), source_ref[box]) for box in range(B_DEV)]
    high, low = split(jnp.concatenate(ups, axis=1))
    both = jnp.concatenate([high, low], axis=0)
    for copy, (start, width), part in zip(copies[5:], SLABS[1:] + SLABS[:1], [*parts, first_ref]):
        copy.wait()
        sums = dot(both, part[pl.ds(0, ROWS)])
        made = (sums[:RANK] + sums[RANK:]).astype(jnp.bfloat16)
        panel_ref[pl.ds(0, RANK), pl.ds(start, width)] = made
        plain_ref[:, pl.ds(start, width)] = made


def up(members, carried, *given):
    columns = given[5].shape[1]
    shapes = [(ROWS, width) for _, width in SLABS]
    shapes[CARRIER] = (ROWS + RANK * -(-carried // shapes[CARRIER][1]), shapes[CARRIER][1])
    return pl.pallas_call(
        functools.partial(up_kernel, members),
        in_specs=[ANYWHERE] * len(given),
        out_shape=(
            jax.ShapeDtypeStruct((RANK + WISH, columns), jnp.bfloat16),
            jax.ShapeDtypeStruct((RANK, columns), jnp.bfloat16),
            jax.ShapeDtypeStruct((B_DEV, NEAR), jnp.int32),
            *[jax.ShapeDtypeStruct(shape, jnp.bfloat16) for shape in shapes[1:]],
        ),
        scratch_shapes=[pltpu.VMEM(a.shape, a.dtype) for a in (*given[:5], given[6])]
        + [pltpu.SemaphoreType.DMA((5 + len(SLABS),))],
        compiler_params=pltpu.CompilerParams(vmem_limit_bytes=UP_LIMIT * MIB),
        cost_estimate=cost(COSTS[0]),
        name="up",
    )(*given)


def down_kernel(reach, members, far_ref, target_ref, leaf_ref, mid_ref, coupling_ref, *rest):
    part_ref, down_ref, placed_ref, lines_ref, sem = rest[-5:]
    for box in range(B_DEV):
        chain = dot(mid_ref[box // 2], leaf_ref[box])
        high, low = split(dot_split(chain, target_ref[box]).T)
        down_ref[box] = jnp.concatenate([high, low, high], axis=1)
    position = lax.axis_index("pts")
    quad, side, core = position >> 2, (position >> 1) & 1, position & 1
    for half in range(2):
        blocks = []
        for other in range(2):
            for step in reach:
                held_quad = quad + step
                held_quad = jnp.where(held_quad >= members // 4, held_quad - members // 4, held_quad)
                group = held_quad * 4 + 2 * (side ^ half) + (core ^ other)
                block = jnp.zeros((RANK, RANK), jnp.float32)
                for f in range(coupling_ref.shape[0]):
                    block = jnp.where(far_ref[0, f] == group, coupling_ref[f].astype(jnp.float32), block)
                blocks.append(block)
        placed = jnp.concatenate(blocks, axis=1).astype(jnp.bfloat16)
        if half == 0:
            placed_ref[...] = placed
            continue
        width = part_ref.shape[1]
        for line, at in enumerate(range(0, placed.shape[1], width)):
            taken = placed[:, at : at + width]
            lines_ref[pl.ds(line * RANK, RANK), pl.ds(0, taken.shape[1])] = taken
        copy = pltpu.make_async_copy(lines_ref, part_ref.at[pl.ds(ROWS, lines_ref.shape[0])], sem)
        copy.start()
        copy.wait()


def down(reach, members, far_ids, target_basis, leaf_transfer, mid_transfer, coupling, part, *before):
    return pl.pallas_call(
        functools.partial(down_kernel, reach, members),
        in_specs=[SCALAR] + [VECTOR] * 4 + [ANYWHERE] + [VECTOR] * len(before),
        out_specs=(ANYWHERE, VECTOR, VECTOR),
        out_shape=(
            jax.ShapeDtypeStruct(part.shape, part.dtype),
            jax.ShapeDtypeStruct((B_DEV, LEAF, 3 * RANK), jnp.bfloat16),
            jax.ShapeDtypeStruct((RANK, 2 * len(reach) * RANK), jnp.bfloat16),
        ),
        scratch_shapes=[
            pltpu.VMEM((part.shape[0] - ROWS, part.shape[1]), part.dtype),
            pltpu.SemaphoreType.DMA,
        ],
        input_output_aliases={5: 0},
        compiler_params=pltpu.CompilerParams(vmem_limit_bytes=16 * MIB),
        cost_estimate=cost(COSTS[1]),
        name="down",
    )(far_ids, target_basis, leaf_transfer, mid_transfer, coupling, part, *before)


def ask_kernel(panel_ref, ahead_ref, behind_ref, *rest):
    asked_ref = rest[-1]
    forth = (lax.axis_index("pts") & 2) == 0
    wishes = (pl.ds(RANK, WISH), pl.ds(0, 6 * 128))
    ahead, behind = ahead_ref[wishes].astype(jnp.float32), behind_ref[wishes].astype(jnp.float32)
    asked_ref[pl.ds(0, WISH)] = jnp.where(forth, ahead, behind).astype(jnp.bfloat16)
    asked_ref[pl.ds(WISH, WISH)] = panel_ref[wishes]


def ask(panel, ahead, behind, *before):
    return pl.pallas_call(
        ask_kernel,
        in_specs=[VECTOR] * 3 + [ANYWHERE] * len(before),
        out_shape=jax.ShapeDtypeStruct((2 * WISH, 6 * 128), jnp.bfloat16),
        compiler_params=pltpu.CompilerParams(vmem_limit_bytes=8 * MIB),
        cost_estimate=cost(0.1),
        name="ask",
    )(panel, ahead, behind, *before)


def wishes_kernel(asked_ref, core_asked_ref, wish_ref):
    for name in range(6):
        ref = asked_ref if name < 2 else core_asked_ref
        value = ref[pl.ds(0 if name < 4 else WISH, WISH), pl.ds(name * 128, 128)]
        wish_ref[0, name] = jnp.max(value.astype(jnp.float32)).astype(jnp.int32)


def wishes(asked, core_asked):
    return pl.pallas_call(
        wishes_kernel,
        in_specs=[VECTOR] * 2,
        out_specs=SCALAR,
        out_shape=jax.ShapeDtypeStruct((1, 6), jnp.int32),
        compiler_params=pltpu.CompilerParams(vmem_limit_bytes=8 * MIB),
        cost_estimate=cost(0.1),
        name="wishes",
    )(asked, core_asked)


def join_kernel(*refs):
    refs[-1][...] = jnp.zeros_like(refs[-1])


def join(microseconds, *values):
    return pl.pallas_call(
        join_kernel,
        in_specs=[ANYWHERE] * len(values),
        out_shape=jax.ShapeDtypeStruct((8, 128), jnp.float32),
        compiler_params=pltpu.CompilerParams(vmem_limit_bytes=MIB),
        cost_estimate=cost(microseconds),
        name="join",
    )(*values)


def couple_kernel(own_ref, carrier_ref, core_ref, *rest):
    panels, (own_sum_ref, partner_sum_ref) = rest[:-2], rest[-2:]
    depth = own_ref.shape[1]
    lines = [core_ref[pl.ds(row, depth // 2)] for row in range(2 * LEAF, core_ref.shape[0], depth // 2)]
    table = [ref[pl.ds(0, RANK)] for ref in panels] + [jnp.concatenate(lines, axis=1)]
    table = jnp.concatenate(table, axis=0)
    lines = [carrier_ref[pl.ds(row, RANK)] for row in range(ROWS, carrier_ref.shape[0], RANK)]
    partner_sum = dot(jnp.concatenate(lines, axis=1)[:, :depth], table)
    partner_sum_ref[...] = partner_sum.astype(jnp.bfloat16)
    own_sum_ref[...] = dot(own_ref[...], table)


def couple(own, carrier, core, *panels):
    shape = (RANK, panels[0].shape[1])
    return pl.pallas_call(
        couple_kernel,
        out_shape=(jax.ShapeDtypeStruct(shape, jnp.float32), jax.ShapeDtypeStruct(shape, jnp.bfloat16)),
        compiler_params=pltpu.CompilerParams(vmem_limit_bytes=16 * MIB),
        cost_estimate=cost(COSTS[6]),
        name="couple",
    )(own, carrier, core, *panels)


def pick(wish_ref, at, arrived_ref, picked_ref):
    for k in range(2):
        rows = pl.ds(pl.multiple_of(wish_ref[0, at + k] * LEAF, LEAF), LEAF)
        picked_ref[pl.ds(k * LEAF, LEAF)] = arrived_ref[rows]


def pack_kernel(panels, wish_ref, arrived_ref, *rest):
    for at, picked_ref in enumerate(rest[-3:]):
        pick(wish_ref, 2 * at, arrived_ref, picked_ref)
    to = 2 * LEAF
    for at in range(0, rest[0].shape[1] if panels else 0, arrived_ref.shape[1]):
        for ref in rest[:panels]:
            rest[-1][pl.ds(to, RANK)] = ref[pl.ds(0, RANK), pl.ds(at, arrived_ref.shape[1])]
            to += RANK


def pack(wish, arrived, panels, before):
    width = arrived.shape[1]
    shape = jax.ShapeDtypeStruct((2 * LEAF, width), arrived.dtype)
    further = sum(RANK * panel.shape[1] // width for panel in panels)
    return pl.pallas_call(
        functools.partial(pack_kernel, len(panels)),
        in_specs=[SCALAR] + [VECTOR] * (1 + len(panels)) + [ANYWHERE] * len(before),
        out_shape=(shape, shape, jax.ShapeDtypeStruct((2 * LEAF + further, width), arrived.dtype)),
        compiler_params=pltpu.CompilerParams(vmem_limit_bytes=8 * MIB),
        cost_estimate=cost(COSTS[5]),
        name="pack",
    )(wish, arrived, *panels, *before)


def gather(start, width, held, pieces):
    own_ref, core_ref, across_ref, across_core_ref, along_ref, along_core_ref = pieces
    for at, boxes, taken in (
        (OWN, B_DEV, own_ref[pl.ds(0, ROWS)]),
        (CORE, B_DEV, core_ref[:, pl.ds(start, width)]),
        (ACROSS, B_DEV, across_ref[pl.ds(0, ROWS)]),
        (ACROSS_CORE, 2, across_core_ref[pl.ds(0, 2 * LEAF)]),
        (ALONG, 2, along_ref[...]),
        (ALONG_CORE, 2, along_core_ref[...]),
    ):
        held[pl.ds(at * LEAF, boxes * LEAF)] = taken
    held[pl.ds(ZERO * LEAF, LEAF)] = jnp.zeros((LEAF, width), jnp.bfloat16)


def operands(box, entry_ref, near_ref, held):
    left = [near_ref[box, n] for n in range(NEAR)]
    right = [held[pl.ds(pl.multiple_of(entry_ref[box, n] * LEAF, LEAF), LEAF)] for n in range(NEAR)]
    return left, right


def near_kernel(start, entry_ref, near_ref, *rest):
    pieces, (sum_ref, held) = rest[:6], rest[-2:]
    gather(start, sum_ref.shape[1], held, pieces)
    for box in range(B_DEV):
        left, right = operands(box, entry_ref, near_ref, held)
        sum_ref[pl.ds(box * LEAF, LEAF)] = dot(
            jnp.concatenate(left, axis=1), jnp.concatenate(right, axis=0)
        )


def near(start, width, entry, near_blocks, pieces, before):
    return pl.pallas_call(
        functools.partial(near_kernel, start),
        in_specs=[SCALAR] + [VECTOR] * (1 + len(pieces)) + [ANYWHERE] * len(before),
        out_specs=VECTOR,
        scratch_shapes=[pltpu.VMEM((HELD * LEAF, width), jnp.bfloat16)],
        out_shape=jax.ShapeDtypeStruct((ROWS, width), jnp.float32),
        compiler_params=pltpu.CompilerParams(vmem_limit_bytes=16 * MIB),
        cost_estimate=cost(COSTS[2]),
        name="near",
    )(entry, near_blocks, *pieces, *before)


def last_kernel(start, width, entry_ref, near_ref, own_sum_ref, partner_sum_ref, down_ref, *rest):
    pieces, (out_ref, held, made, sems) = rest[:6], rest[-4:]
    gather(start, width, held, pieces)
    taken = pl.ds(start, width)
    high, low = split(own_sum_ref[:, taken] + partner_sum_ref[:, taken].astype(jnp.float32))
    coupled = jnp.concatenate([high, high, low], axis=0)
    copies = []
    for box in range(B_DEV):
        left, right = operands(box, entry_ref, near_ref, held)
        rows = pl.ds(box * LEAF, LEAF)
        near_sum = dot(jnp.concatenate(left, axis=1), jnp.concatenate(right, axis=0))
        made[rows] = (near_sum + dot(down_ref[box], coupled)).astype(jnp.bfloat16)
        copy = pltpu.make_async_copy(made.at[rows], out_ref.at[rows, taken], sems.at[box])
        copy.start()
        copies.append(copy)
    for copy in copies:
        copy.wait()


def last(start, width, entry, near_blocks, sums, down_basis, pieces, mark, product):
    given = [entry, near_blocks, *sums, down_basis, *pieces, mark, product]
    return pl.pallas_call(
        functools.partial(last_kernel, start, width),
        in_specs=[SCALAR] + [VECTOR] * (len(given) - 3) + [ANYWHERE] * 2,
        out_specs=ANYWHERE,
        scratch_shapes=[
            pltpu.VMEM((HELD * LEAF, width), jnp.bfloat16),
            pltpu.VMEM((ROWS, width), jnp.bfloat16),
            pltpu.SemaphoreType.DMA((B_DEV,)),
        ],
        out_shape=jax.ShapeDtypeStruct(product.shape, product.dtype),
        input_output_aliases={len(given) - 1: 0},
        compiler_params=pltpu.CompilerParams(vmem_limit_bytes=16 * MIB),
        cost_estimate=cost(COSTS[4]),
        name="last",
    )(*given)


def finish_kernel(slabs, own_sum_ref, partner_sum_ref, down_ref, *rest):
    sum_refs = rest[: len(slabs)]
    out_ref, made, sems = rest[-3:]
    start, stop = slabs[0][0], slabs[-1][0] + slabs[-1][1]
    taken = pl.ds(start, stop - start)
    high, low = split(own_sum_ref[:, taken] + partner_sum_ref[:, taken].astype(jnp.float32))
    coupled = jnp.concatenate([high, high, low], axis=0)
    copies = []
    for box in range(B_DEV):
        rows = pl.ds(box * LEAF, LEAF)
        far = dot(down_ref[box], coupled)
        for (at, width), sum_ref in zip(slabs, sum_refs):
            columns = slice(at - start, at - start + width)
            made[rows, columns] = (far[:, columns] + sum_ref[rows]).astype(jnp.bfloat16)
        copy = pltpu.make_async_copy(made.at[rows], out_ref.at[rows, taken], sems.at[box])
        copy.start()
        copies.append(copy)
    for copy in copies:
        copy.wait()


def finish(slabs, sums, down_basis, nears):
    columns = sums[0].shape[1]
    given = [*sums, down_basis, *nears]
    return pl.pallas_call(
        functools.partial(finish_kernel, slabs),
        in_specs=[VECTOR] * len(given),
        out_specs=ANYWHERE,
        scratch_shapes=[
            pltpu.VMEM((ROWS, sum(width for _, width in slabs)), jnp.bfloat16),
            pltpu.SemaphoreType.DMA((B_DEV,)),
        ],
        out_shape=jax.ShapeDtypeStruct((ROWS, columns), jnp.bfloat16),
        compiler_params=pltpu.CompilerParams(vmem_limit_bytes=16 * MIB),
        cost_estimate=cost(COSTS[3]),
        name="finish",
    )(*given)


def on_device(
    rhs,
    near_blocks,
    near_ids,
    near_count,
    source_basis,
    target_basis,
    leaf_transfer,
    mid_transfer,
    far_coupling,
    far_ids,
):
    members = lax.axis_size("pts")
    every = range(members)
    across_pairs = [(i, i ^ 2) for i in every]
    core_pairs = [(i, i ^ 1) for i in every]
    along_pairs = [(i, (i + (-4 if i & 2 else 4)) % members) for i in every]
    along_core_pairs = [(i, (i + (-3 if i & 2 else 3)) % members) for i in every if i % 4 in (1, 2)]
    permute = lambda value, pairs: lax.ppermute(value, "pts", pairs)
    meet = lambda *values: lax.optimization_barrier(values)
    quads = members // 4
    reach = list(dict.fromkeys(step % quads for step in (0, 1, -1, 2, -2)))

    rhs_core = permute(rhs, core_pairs)
    first = rhs[:, : SLABS[0][1]]
    panel, plain, entry, *parts = up(
        members,
        2 * len(reach) * RANK,
        source_basis,
        leaf_transfer,
        mid_transfer,
        near_ids,
        near_count.reshape(1, B_DEV),
        rhs,
        first,
    )
    parts = [first, *parts]
    parts[CARRIER], down_basis, placed = down(
        reach, members, far_ids, target_basis, leaf_transfer, mid_transfer, far_coupling[0], parts[CARRIER], panel
    )
    across = [permute(part, across_pairs) for part in parts[:3]]
    back = lambda step: [(i, (i - 4 * step) % members) for i in every]
    others = [permute(panel, back(step)) for step in reach[1:3]]
    others += [permute(plain, back(step)) for step in reach[3:]]
    across[0], panel, others[0], others[1] = meet(across[0], panel, others[0], others[1])
    asked = ask(panel, others[0], others[1], rhs_core, down_basis)
    wish = wishes(asked, permute(asked, core_pairs))

    nears, along, across_core = [], [], []

    def marked(microseconds, *values):
        return [join(microseconds, *values)] if microseconds else []

    def pieces(k):
        return (parts[k], rhs_core, across[k], across_core[k], *along[k])

    for k in range(len(SLABS)):
        if k >= 2:
            nears.append(near(*SLABS[k - 2], entry, near_blocks, pieces(k - 2), nears[-1:] + marked(ZJ[k - 2], *along[k - 2])))
        panels = [panel, *others] if k == PK else []
        before = nears[-1:] + marked(XJ[k], across[k])
        if k and XC[k - 1]:
            before.append(across_core[k - 1])
        picks = list(pack(wish, across[k], panels, before))
        along.append([permute(picks[0], along_pairs), permute(picks[1], along_core_pairs)])
        if k and MC[k - 1]:
            picks[2], along[k - 1][0] = meet(picks[2], along[k - 1][0])
        across_core.append(permute(picks[2], core_pairs))
        if k == 1:
            if M3:
                parts[3], along[0][M3 - 1] = meet(parts[3], along[0][M3 - 1])
            across.append(permute(parts[3], across_pairs))
    own_sum, partner_sum = couple(placed, across[CARRIER], across_core[PK], panel, *others)
    sums = (own_sum, permute(partner_sum, across_pairs))
    nears.append(near(*SLABS[2], entry, near_blocks, pieces(2), nears[-1:] + marked(ZJ[2], *along[2])))
    product = finish(SLABS[:-1], sums, down_basis, nears)
    return last(*SLABS[-1], entry, near_blocks, sums, down_basis, pieces(3), join(ZJ[3], *along[3]), product)


def solution(mesh):
    return jax.shard_map(
        on_device,
        mesh=mesh,
        in_specs=(
            P(("parts", "pts"), None),
            P(("parts", "pts"), None, None, None),
            P(("parts", "pts"), None),
            P(("parts", "pts")),
            P(("parts", "pts"), None, None),
            P(("parts", "pts"), None, None),
            P(("parts", "pts"), None, None),
            P(("parts", "pts"), None, None),
            P(("parts", "pts"), None, None, None),
            P(("parts", "pts"), None),
        ),
        out_specs=P(("parts", "pts"), None),
        check_vma=False,
    )
```
